128 devices in a mesh: seq: 8 (over z, core), tensor: 16 (over y, x).
Axes of the slice: x: 4, y: 4, z: 4, core: 2. Of those that a mesh axis runs over, the one named last changes fastest.
Arguments:
- tokens: bfloat16 [6144, 8192], P('seq', 'tensor'), may hold values from -6 to 6
- cotangent: bfloat16 [6144, 10240], P('seq', 'tensor'), may hold values from -6 to 6
- gates: float32 [6144, 4], P('seq'), may hold values from 0.25 to 1
- weight: bfloat16 [8192, 10240], P(None, 'tensor'), may hold values from -0.09375 to 0.09375
- adapter_down_store: bfloat16 [1024, 16, 8192], P('seq', None, 'tensor'), may hold values from -0.0625 to 0.0625
- adapter_up_store: bfloat16 [1024, 16, 10240], P('seq', None, 'tensor'), may hold values from -1.5 to 1.5
- expert_per_group: int32 [8, 4], replicated, may hold values from 0 to 1023, as said below
- adapter_store_row: int32 [1024], replicated, may hold values from 0 to 1023, as said below
Outputs:
- projected: bfloat16 [6144, 10240], P('seq', 'tensor')
- grad_tokens: bfloat16 [6144, 8192], P('seq', 'tensor')
The draws below stay inside these ranges and needn't reach their ends.
Inputs may be any that keep to these rules, and one draw needn't show every extreme that they name: `expert_per_group`: each row names 4 different adapters; at most 2 of a row's adapters have adapter_store_row // 128 equal, and some row has exactly 2 so. `adapter_store_row`: A permutation of the adapters.
All inputs are finite; a program needn't handle non-finite values.
Results may differ from the reference program's by a relative error of at most 0.004.
Values may be sent and summed in bfloat16 or wider, within the bound.
A program may use at most 192 MiB of HBM per device.

```python
import jax
import jax.numpy as jnp

MODEL_WIDTH = 8192
ADAPTER_RANK = 16
TOPE = 4
TOK_GRP = 768
EXP_ROW = 128
PROJECTION_COLS = 10240
GROUPS = 8
TOKENS = 6144
ADAPTER_TOTAL = 1024


def swap_labels(chosen, placed, first, second):
    relabel = lambda values: jnp.where(values == first, second, jnp.where(values == second, first, values))
    ids = jnp.arange(ADAPTER_TOTAL, dtype=jnp.int32)
    return (relabel(chosen).astype(jnp.int32), jnp.take(placed, relabel(ids), axis=0).astype(jnp.int32))


def shared_tables(key):
    keys = jax.random.split(key, 7)
    placed = jax.random.permutation(keys[0], ADAPTER_TOTAL).astype(jnp.int32)
    holder = jnp.zeros((ADAPTER_TOTAL,), jnp.int32).at[placed].set(jnp.arange(ADAPTER_TOTAL, dtype=jnp.int32))
    group_keys = jax.random.split(keys[1], GROUPS)
    owners = jax.vmap(lambda k: jax.random.permutation(k, GROUPS))(group_keys).astype(jnp.int32)
    first_pair = jax.random.randint(keys[2], (GROUPS,), 0, 2).at[0].set(1)
    second_pair = jax.random.randint(keys[3], (GROUPS,), 0, 2)
    holders = jnp.stack([owners[:, 0], jnp.where(first_pair == 1, owners[:, 0], owners[:, 3]), owners[:, 1], jnp.where(second_pair == 1, owners[:, 1], owners[:, 2])], axis=1)
    slots = jax.random.randint(keys[4], (GROUPS, 4), 0, EXP_ROW)
    steps = jax.random.randint(keys[5], (GROUPS, 2), 1, EXP_ROW)
    slot_b = jnp.where(first_pair == 1, (slots[:, 0] + steps[:, 0]) % EXP_ROW, slots[:, 1])
    slot_d = jnp.where(second_pair == 1, (slots[:, 2] + steps[:, 1]) % EXP_ROW, slots[:, 3])
    slots = jnp.stack([slots[:, 0], slot_b, slots[:, 2], slot_d], axis=1)
    order_keys = jax.random.split(keys[6], GROUPS)
    orders = jax.vmap(lambda k: jax.random.permutation(k, 4))(order_keys).astype(jnp.int32)
    row_indices = holders * EXP_ROW + slots
    row_indices = jnp.take_along_axis(row_indices, orders, axis=1)
    chosen = jnp.take(holder, row_indices, axis=0).astype(jnp.int32)
    chosen, placed = swap_labels(chosen, placed, chosen[0, 0], jnp.int32(ADAPTER_TOTAL - 1))
    chosen, placed = swap_labels(chosen, placed, chosen[0, 1], jnp.int32(0))
    return (chosen.astype(jnp.int32), placed)


def draw_expert_per_group(key, part):
    return shared_tables(key)[0]


def draw_adapter_store_row(key, part):
    return shared_tables(key)[1]


def raised(array, own_key, source, target, blocks, factor):
    def block_of(dim):
        return (jnp.arange(array.shape[dim]) // (array.shape[dim] // blocks)).reshape((-1,) + (1,) * (array.ndim - 1 - dim))

    first = jax.random.permutation(own_key, blocks)[block_of(target)]
    far = (block_of(target) + blocks // 2) % blocks
    return jnp.where((block_of(source) == first) | (block_of(source) == far), factor * array, array)


def steps_of(stream_key, shape, cuts, smallest, top_value):
    loudness = 1.0
    for dim, shards_of in cuts:
        draws = jax.random.uniform(jax.random.fold_in(jax.random.fold_in(stream_key, 6), dim), (shards_of,), jnp.float32, smallest / len(cuts), top_value / len(cuts))
        loudness = loudness * jnp.repeat(jnp.exp(draws), shape[dim] // shards_of).reshape((-1,) + (1,) * (len(shape) - 1 - dim))
    return loudness


def scatter_about(rng, dims, deviation, bound, pieces=(), kind=jnp.bfloat16):
    values = jax.random.normal(rng, dims, jnp.float32) * deviation
    if len(pieces) > 0:
        values = steps_of(rng, dims, pieces, -0.22, 0.18) * values
    return jnp.clip(values, min=-bound, max=bound).astype(kind)


def gaussian_with(own_key, shape, width, most, cuts, heavy, held_as=jnp.bfloat16):
    drawn = width * jax.random.normal(own_key, shape, jnp.float32)
    if cuts:
        drawn = drawn * steps_of(own_key, shape, cuts, -0.22, 0.18)
    return jnp.clip(raised(drawn, jax.random.fold_in(own_key, 3), *heavy), -most, most).astype(held_as)


def setup_inputs(seed: int = 0) -> dict:
    seeds = jax.random.split(jax.random.key(seed), 9)
    tokens = scatter_about(seeds[0], (TOKENS, MODEL_WIDTH), 1.0, 6.0, ((0, 8), (1, 16)))
    cotangent = scatter_about(seeds[1], (TOKENS, PROJECTION_COLS), 1.0, 6.0, ((0, 8), (1, 16)))
    gates = jnp.clip(0.25 + 0.75 * jax.random.uniform(seeds[2], (TOKENS, TOPE), jnp.float32) ** steps_of(seeds[2], (TOKENS, TOPE), ((0, 8),), -0.2, 0.2), 0.25, 1.0)
    weight = gaussian_with(seeds[3], (MODEL_WIDTH, PROJECTION_COLS), MODEL_WIDTH ** -0.5, 0.09375, ((1, 16),), (1, 0, 16, 2.0))
    adapter_down_store = scatter_about(seeds[4], (ADAPTER_TOTAL, ADAPTER_RANK, MODEL_WIDTH), MODEL_WIDTH ** -0.5, 0.0625, ((0, 8), (2, 16)))
    adapter_up_store = scatter_about(seeds[5], (ADAPTER_TOTAL, ADAPTER_RANK, PROJECTION_COLS), ADAPTER_RANK ** -0.5, 1.5, ((0, 8), (2, 16)))
    expert_per_group = draw_expert_per_group(jax.random.fold_in(seeds[8], 71), 0)
    adapter_store_row = draw_adapter_store_row(jax.random.fold_in(seeds[8], 71), 0)
    return {"tokens": tokens, "cotangent": cotangent, "gates": gates, "weight": weight, "adapter_down_store": adapter_down_store, "adapter_up_store": adapter_up_store, "expert_per_group": expert_per_group, "adapter_store_row": adapter_store_row}


def reference(tokens, cotangent, gates, weight, adapter_down_store, adapter_up_store, expert_per_group, adapter_store_row):
    projected = []
    grad_tokens = []
    for group in range(GROUPS):
        row_indices = jnp.take(adapter_store_row, expert_per_group[group], axis=0).astype(jnp.int32)
        down_matrix = jnp.take(adapter_down_store, row_indices, axis=0).astype(jnp.float32)
        upper_matrix = jnp.take(adapter_up_store, row_indices, axis=0).astype(jnp.float32)
        start = group * TOK_GRP
        inputs = tokens[start:start + TOK_GRP]
        outgrad = cotangent[start:start + TOK_GRP]
        mixing = gates[start:start + TOK_GRP]
        low = jnp.einsum('td,jrd->tjr', inputs.astype(jnp.float32), down_matrix)
        low_gated = (low * mixing[:, :, None]).astype(jnp.bfloat16)
        result = jnp.dot(inputs, weight, preferred_element_type=jnp.float32)
        result = result + jnp.einsum('tjr,jrc->tc', low_gated.astype(jnp.float32), upper_matrix)
        projected.append(result.astype(jnp.bfloat16))
        back = jnp.einsum('tc,jrc->tjr', outgrad.astype(jnp.float32), upper_matrix)
        back_gated = (back * mixing[:, :, None]).astype(jnp.bfloat16)
        gradient = jnp.dot(outgrad, weight.T, preferred_element_type=jnp.float32)
        gradient = gradient + jnp.einsum('tjr,jrd->td', back_gated.astype(jnp.float32), down_matrix)
        grad_tokens.append(gradient.astype(jnp.bfloat16))
    return (jnp.concatenate(projected, axis=0), jnp.concatenate(grad_tokens, axis=0))
```

```python
import jax
import jax.numpy as jnp
from jax import lax
from jax.experimental import pallas as pl
from jax.experimental.pallas import tpu as pltpu
from jax.sharding import PartitionSpec as P

F32 = jnp.float32
BF16 = jnp.bfloat16
MESH = pl.DeviceIdType.MESH
RING = 4
CORES = 2
GROUP = 768
HALF = GROUP // 2
FEATS = 512
COLS = 640
ROW_FEATS = RING * FEATS
ROW_COLS = RING * COLS
RANK = 16
USED = 4
LOW = USED * RANK
STORED = 128
SEQ = RING * CORES
CAP = 2
PIECE = FEATS // CORES
PART = PIECE // 2
CHUNKS = 3
CHUNK = HALF // CHUNKS
TRANSPOSED = (((1,), (1,)), ((), ()))
N_SEMS = 128


def ds(start, size, align):
    return pl.ds(pl.multiple_of(start, align), size)


def kernel(
    tok, cot, gates, weight, down, up, expert, store_row,
    projected, grad_tokens,
    wg, tok_g, cot_g, gate_v, down_v, up_v, ad_send, ad_recv, dd, uu, low_hl, back_hl,
    y_far, y_plus, y_minus, y_keep, y_own, y_relay, y_in, y_out,
    x_far, x_plus, x_minus, x_keep, x_own, x_relay, x_in, x_out,
    local_sem, send_sem, recv_sem,
):
    seq, ten = lax.axis_index("seq"), lax.axis_index("tensor")
    z, c = seq // CORES, lax.rem(seq, CORES)
    y, x = ten // RING, lax.rem(ten, RING)

    def ring(value, step):
        return lax.rem(value + (step + RING), RING)

    def at_x(step):
        return (seq, y * RING + ring(x, step))

    def at_y(step):
        return (seq, ring(y, step) * RING + x)

    def at_z(step):
        return (ring(z, step) * CORES + c, ten)

    other_core = (z * CORES + (1 - c), ten)

    def at_seq(step):
        return (lax.rem(seq + step, SEQ), ten)

    barrier = pltpu.get_barrier_semaphore()
    partners = [at_x(s) for s in (1, 2, 3)] + [at_y(s) for s in (1, 2, 3)]
    partners += [at_seq(s) for s in range(1, SEQ)]
    for partner in partners:
        pl.semaphore_signal(barrier, inc=1, device_id=partner, device_id_type=MESH)

    rows_y = ds(y * ROW_FEATS, ROW_FEATS, ROW_FEATS)
    cols_x = ds(x * FEATS, FEATS, 128)
    cols_y = ds(y * COLS, COLS, 128)
    loads = [
        (down, down_v), (up, up_v), (gates, gate_v),
        (tok, tok_g.at[:, cols_x]), (cot, cot_g.at[:, cols_y]),
        (weight.at[rows_y, :], wg.at[:, cols_y]),
    ]
    loads = [pltpu.make_async_copy(s, d, local_sem.at[i]) for i, (s, d) in enumerate(loads)]
    for load in loads:
        load.start()

    started = []
    names = {}

    def remote(name, src, dst, device):
        i = names.setdefault(name, len(names))
        copy = pltpu.make_async_remote_copy(
            src_ref=src, dst_ref=dst, send_sem=send_sem.at[i], recv_sem=recv_sem.at[i],
            device_id=device, device_id_type=MESH,
        )
        copy.start()
        started.append(copy)
        return copy

    pl.semaphore_wait(barrier, len(partners))

    my_rows = ds(z * FEATS + c * PIECE, PIECE, PIECE)
    w_in = {}
    for step in (2, 1, 3):
        first = ring(y, step) * ROW_FEATS + z * FEATS + c * PIECE
        w_in[step] = remote(
            ("w", step), weight.at[ds(first, PIECE, PIECE), :], wg.at[my_rows, cols_y], at_y(step)
        )

    H = (pl.ds(0, HALF), pl.ds(HALF, HALF))

    def gather_first(name, src, dst, cols, at):
        return (
            remote((name, "p0"), src.at[H[0], :], dst.at[H[0], cols], at(1)),
            remote((name, "m1"), src.at[H[1], :], dst.at[H[1], cols], at(-1)),
        )

    def gather_second(name, src, dst, cols, at):
        return (
            remote((name, "p1"), src.at[H[1], :], dst.at[H[1], cols], at(1)),
            remote((name, "m0"), src.at[H[0], :], dst.at[H[0], cols], at(-1)),
        )

    def gather_relay(name, first, dst, pos, width, at):
        first[0].wait_recv()
        from_left = dst.at[H[0], ds(ring(pos, -1) * width, width, 128)]
        a = remote((name, "r0"), from_left, from_left, at(1))
        first[1].wait_recv()
        from_right = dst.at[H[1], ds(ring(pos, 1) * width, width, 128)]
        b = remote((name, "r1"), from_right, from_right, at(-1))
        return a, b

    tok_first = gather_first("tok", tok, tok_g, cols_x, at_x)
    tok_second = gather_second("tok", tok, tok_g, cols_x, at_x)
    cot_first = gather_first("cot", cot, cot_g, cols_y, at_y)

    loads[0].wait()
    loads[1].wait()

    def fill(g, carry):
        picks = [jnp.int32(0)] * CAP
        count = jnp.int32(0)
        for j in range(USED):
            local = store_row[expert[g, j]] - seq * STORED
            mine = (local >= 0) & (local < STORED)
            for k in range(CAP):
                picks[k] = jnp.where(mine & (count == k), local, picks[k])
            count = count + mine.astype(jnp.int32)
        for k in range(CAP):
            ad_send[g * CAP + k, :, :FEATS] = down_v[picks[k]]
            ad_send[g * CAP + k, :, FEATS:] = up_v[picks[k]]
        return carry

    lax.fori_loop(0, SEQ, fill, 0)
    mine_slots = pl.ds(seq * CAP, CAP)
    ad_in = []
    for step in range(1, SEQ):
        target = at_seq(step)
        ad_in.append(
            remote(("ad", step), ad_send.at[pl.ds(target[0] * CAP, CAP)], ad_recv.at[mine_slots], target)
        )
    for k in range(CAP):
        ad_recv[seq * CAP + k] = ad_send[seq * CAP + k]

    core_in = []

    def to_core(name, place):
        core_in.append((name[1], remote(name, place, place, other_core)))

    def z_place(zz, q, part=None):
        first = zz * FEATS + c * PIECE + (0 if part is None else part * PART)
        return wg.at[ds(first, PIECE if part is None else PART, PART), ds(q * COLS, COLS, 128)]

    def z_start(step):
        w_in[step].wait_recv()
        q = ring(y, -step)
        n = lambda k: ("z", step, k)
        out = {}
        for part in (0, 1):
            here = z_place(z, q, part)
            out["p", part] = remote(n(("p", part)), here, here, at_z(1))
            here = z_place(z, q, 1 - part)
            out["m", 1 - part] = remote(n(("m", 1 - part)), here, here, at_z(-1))
        to_core(("core", step, 0), z_place(z, q))
        return out

    def z_relay(step, out):
        q = ring(y, -step)
        out["p", 0].wait_recv()
        here = z_place(ring(z, -1), q, 0)
        out["r", 0] = remote(("z", step, "r0"), here, here, at_z(1))
        out["m", 1].wait_recv()
        here = z_place(ring(z, 1), q, 1)
        out["r", 1] = remote(("z", step, "r1"), here, here, at_z(-1))

    def z_near(step, out):
        q = ring(y, -step)
        out["p", 1].wait_recv()
        to_core(("core", step, 3), z_place(ring(z, -1), q))
        out["m", 0].wait_recv()
        to_core(("core", step, 1), z_place(ring(z, 1), q))

    def z_far(step, out):
        q = ring(y, -step)
        out["r", 0].wait_recv()
        out["r", 1].wait_recv()
        to_core(("core", step, 2), z_place(ring(z, 2), q))

    def core_wait(step):
        for s, copy in core_in:
            if s == step:
                copy.wait_recv()

    z2 = z_start(2)
    tok_relay = gather_relay("tok", tok_first, tok_g, x, FEATS, at_x)

    for copy in ad_in:
        copy.wait_recv()
    holders = []
    for j in range(USED):
        holder = store_row[expert[seq, j]] // STORED
        rank = jnp.int32(0)
        for earlier in holders:
            rank = rank + (earlier == holder).astype(jnp.int32)
        holders.append(holder)
        rows = ad_recv[holder * CAP + rank]
        dd[pl.ds(j * RANK, RANK), cols_x] = rows[:, :FEATS]
        uu[pl.ds(j * RANK, RANK), cols_y] = rows[:, FEATS:]
    low_rows = pl.ds(0, LOW)
    up_in = []
    down_in = []
    for step in (2, 1, 3):
        here = uu.at[low_rows, cols_y]
        up_in.append(remote(("up", step), here, here, at_y(step)))
        here = dd.at[low_rows, cols_x]
        down_in.append(remote(("down", step), here, here, at_x(step)))
    cot_second = gather_second("cot", cot, cot_g, cols_y, at_y)

    z_relay(2, z2)
    z3 = z_start(3)
    z1 = z_start(1)
    z_near(2, z2)
    z_far(2, z2)

    loads[2].wait()
    lane = lax.broadcasted_iota(jnp.int32, (GROUP, LOW), 1) // RANK
    gate = jnp.zeros((GROUP, LOW), F32)
    for j in range(USED):
        gate = jnp.where(lane == j, gate_v[:, j : j + 1], gate)

    def split_gated(value, out):
        gated = value * gate
        high = gated.astype(BF16)
        out[:, :LOW] = high
        out[:, LOW:] = (gated - high.astype(F32)).astype(BF16)

    for copy in tok_second + tok_relay:
        copy.wait_recv()
    loads[3].wait()
    cot_relay = gather_relay("cot", cot_first, cot_g, y, COLS, at_y)
    for copy in down_in + up_in:
        copy.wait_recv()
    dd[LOW:, :] = dd[:LOW, :]
    uu[LOW:, :] = uu[:LOW, :]
    split_gated(
        lax.dot_general(tok_g[...], dd[:LOW, :], TRANSPOSED, preferred_element_type=F32), low_hl
    )

    def project(q):
        cols = ds(q * COLS, COLS, 128)
        return jnp.dot(tok_g[...], wg[:, cols], preferred_element_type=F32) + jnp.dot(
            low_hl[...], uu[:, cols], preferred_element_type=F32
        )

    def input_grad(q):
        feats = ds(q * FEATS, FEATS, FEATS)
        return lax.dot_general(
            cot_g[...], wg[feats, :], TRANSPOSED, preferred_element_type=F32
        ) + jnp.dot(
            back_hl[...], dd[:, ds(q * FEATS, FEATS, 128)], preferred_element_type=F32
        )

    def far_send(name, value, far, relay, at):
        far[...] = value.astype(BF16)
        return (
            remote((name, "f0"), far.at[H[0], :], relay.at[0], at(1)),
            remote((name, "f1"), far.at[H[1], :], relay.at[1], at(-1)),
        )

    def near_send(name, value, way, out, keep, arrive, at):
        direct = 1 - way
        out[H[direct], :] = value[direct * HALF : (direct + 1) * HALF].astype(BF16)
        copy = remote(
            (name, "n", way), out.at[H[direct], :], arrive.at[way, H[direct], :], at(1 if way == 0 else -1)
        )
        keep[way] = value[way * HALF : (way + 1) * HALF]
        return copy

    def relay_send(name, far_in, way, out, keep, relay, arrive, at):
        far_in[way].wait_recv()
        copies = []
        for k in range(CHUNKS):
            inner = pl.ds(k * CHUNK, CHUNK)
            outer = pl.ds(way * HALF + k * CHUNK, CHUNK)
            out[outer, :] = (keep[way, inner, :] + relay[way, inner, :].astype(F32)).astype(BF16)
            copies.append(
                remote((name, "s", way, k), out.at[outer, :], arrive.at[way, outer, :], at(1 if way == 0 else -1))
            )
        return copies

    def finish(near, sums, own, arrive, out, result, first_sem):
        near[0].wait_recv()
        near[1].wait_recv()
        copies = []
        for k in range(CHUNKS):
            for way in (0, 1):
                sums[way][k].wait_recv()
                rows = pl.ds(way * HALF + k * CHUNK, CHUNK)
                out[rows, :] = (
                    own[rows, :] + arrive[0, rows, :].astype(F32) + arrive[1, rows, :].astype(F32)
                ).astype(BF16)
                copy = pltpu.make_async_copy(
                    out.at[rows, :], result.at[rows, :], local_sem.at[first_sem + len(copies)]
                )
                copy.start()
                copies.append(copy)
        return copies

    core_wait(2)
    loads[5].wait()
    y_far_in = far_send("y", project(ring(y, 2)), y_far, y_relay, at_y)
    z_relay(3, z3)
    y_own[...] = project(y)
    z_near(3, z3)
    z_relay(1, z1)
    z_near(1, z1)
    z_far(3, z3)
    core_wait(3)
    y_near = {}
    z_far(1, z1)
    core_wait(1)
    y_near[0] = near_send("y", project(ring(y, 1)), 0, y_plus, y_keep, y_in, at_y)
    y_near[1] = near_send("y", project(ring(y, -1)), 1, y_minus, y_keep, y_in, at_y)

    for copy in cot_second + cot_relay:
        copy.wait_recv()
    loads[4].wait()
    split_gated(
        lax.dot_general(cot_g[...], uu[:LOW, :], TRANSPOSED, preferred_element_type=F32), back_hl
    )
    x_far_in = far_send("x", input_grad(ring(x, 2)), x_far, x_relay, at_x)
    x_near = {}
    x_near[0] = near_send("x", input_grad(ring(x, 1)), 0, x_plus, x_keep, x_in, at_x)
    x_near[1] = near_send("x", input_grad(ring(x, -1)), 1, x_minus, x_keep, x_in, at_x)
    x_own[...] = input_grad(x)
    y_sums = [
        relay_send("y", y_far_in, 0, y_plus, y_keep, y_relay, y_in, at_y),
        relay_send("y", y_far_in, 1, y_minus, y_keep, y_relay, y_in, at_y),
    ]
    x_sums = [
        relay_send("x", x_far_in, 0, x_plus, x_keep, x_relay, x_in, at_x),
        relay_send("x", x_far_in, 1, x_minus, x_keep, x_relay, x_in, at_x),
    ]
    last = finish(x_near, x_sums, x_own, x_in, x_out, grad_tokens, len(loads))
    last += finish(y_near, y_sums, y_own, y_in, y_out, projected, len(loads) + 2 * CHUNKS)
    for copy in last:
        copy.wait()
    for copy in started:
        copy.wait_send()


def per_device(tokens, cotangent, gates, weight, down, up, expert, store_row):
    any_space = pl.BlockSpec(memory_space=pl.ANY)
    smem = pl.BlockSpec(memory_space=pltpu.SMEM)

    def ring_scratch(width):
        return [
            pltpu.VMEM((GROUP, width), BF16),
            pltpu.VMEM((GROUP, width), BF16),
            pltpu.VMEM((GROUP, width), BF16),
            pltpu.VMEM((2, HALF, width), F32),
            pltpu.VMEM((GROUP, width), F32),
            pltpu.VMEM((2, HALF, width), BF16),
            pltpu.VMEM((2, GROUP, width), BF16),
            pltpu.VMEM((GROUP, width), BF16),
        ]

    flops = 2 * 2 * GROUP * ROW_FEATS * ROW_COLS
    return pl.pallas_call(
        kernel,
        out_shape=(
            jax.ShapeDtypeStruct((GROUP, COLS), BF16),
            jax.ShapeDtypeStruct((GROUP, FEATS), BF16),
        ),
        in_specs=[any_space] * 6 + [smem] * 2,
        out_specs=(any_space, any_space),
        scratch_shapes=[
            pltpu.VMEM((ROW_FEATS, ROW_COLS), BF16),
            pltpu.VMEM((GROUP, ROW_FEATS), BF16),
            pltpu.VMEM((GROUP, ROW_COLS), BF16),
            pltpu.VMEM((GROUP, USED), F32),
            pltpu.VMEM((STORED, RANK, FEATS), BF16),
            pltpu.VMEM((STORED, RANK, COLS), BF16),
            pltpu.VMEM((SEQ * CAP, RANK, FEATS + COLS), BF16),
            pltpu.VMEM((SEQ * CAP, RANK, FEATS + COLS), BF16),
            pltpu.VMEM((2 * LOW, ROW_FEATS), BF16),
            pltpu.VMEM((2 * LOW, ROW_COLS), BF16),
            pltpu.VMEM((GROUP, 2 * LOW), BF16),
            pltpu.VMEM((GROUP, 2 * LOW), BF16),
        ]
        + ring_scratch(COLS)
        + ring_scratch(FEATS)
        + [
            pltpu.SemaphoreType.DMA((6 + 4 * CHUNKS,)),
            pltpu.SemaphoreType.DMA((N_SEMS,)),
            pltpu.SemaphoreType.DMA((N_SEMS,)),
        ],
        compiler_params=pltpu.CompilerParams(
            collective_id=0, has_side_effects=True, vmem_limit_bytes=60 * 2**20
        ),
        cost_estimate=pl.CostEstimate(flops=flops, bytes_accessed=20 * 2**20, transcendentals=0),
        name="mixture",
    )(tokens, cotangent, gates, weight, down, up, expert, store_row)


def solution(mesh):
    return jax.shard_map(
        per_device,
        mesh=mesh,
        in_specs=(
            P("seq", "tensor"),
            P("seq", "tensor"),
            P("seq", None),
            P(None, "tensor"),
            P("seq", None, "tensor"),
            P("seq", None, "tensor"),
            P(),
            P(),
        ),
        out_specs=(P("seq", "tensor"), P("seq", "tensor")),
        check_vma=False,
    )
```

```python
import jax
import jax.numpy as jnp
from jax import lax
from jax.experimental import pallas as pl
from jax.experimental.pallas import tpu as pltpu
from jax.sharding import PartitionSpec as P

F32 = jnp.float32
BF16 = jnp.bfloat16
MESH = pl.DeviceIdType.MESH
RING = 4
CORES = 2
GROUP = 768
HALF = GROUP // 2
FEATS = 512
COLS = 640
ROW_FEATS = RING * FEATS
ROW_COLS = RING * COLS
RANK = 16
USED = 4
LOW = USED * RANK
STORED = 128
SEQ = RING * CORES
CAP = 2
PIECE = FEATS // CORES
PART = PIECE // 2
CHUNKS = 3
CHUNK = HALF // CHUNKS
TRANSPOSED = (((1,), (1,)), ((), ()))
N_SEMS = 128
COPIES = 4


def ds(start, size, align):
    return pl.ds(pl.multiple_of(start, align), size)


def kernel(
    tok, cot, gates, weight, down, up, expert, store_row,
    projected, grad_tokens,
    wg, tok_g, cot_g, gate_v, gate_t, gate, down_v, up_v, ad_send, ad_recv, dd, uu, low_hl, back_hl,
    back_part, x2_part,
    y_far, y_plus, y_minus, y_keep, y_own, y_relay, y_in, y_out,
    x_far, x_plus, x_minus, x_keep, x_own, x_relay, x_in, x_out,
    local_sem, send_sem, recv_sem,
):
    seq, ten = lax.axis_index("seq"), lax.axis_index("tensor")
    z, c = seq // CORES, lax.rem(seq, CORES)
    y, x = ten // RING, lax.rem(ten, RING)

    def ring(value, step):
        return lax.rem(value + (step + RING), RING)

    def at_x(step):
        return (seq, y * RING + ring(x, step))

    def at_y(step):
        return (seq, ring(y, step) * RING + x)

    def at_z(step):
        return (ring(z, step) * CORES + c, ten)

    other_core = (z * CORES + (1 - c), ten)

    def at_seq(step):
        return (lax.rem(seq + step, SEQ), ten)

    barrier = pltpu.get_barrier_semaphore()
    partners = [at_x(s) for s in (1, 2, 3)] + [at_y(s) for s in (1, 2, 3)]
    partners += [at_seq(s) for s in range(1, SEQ)]
    for partner in partners:
        pl.semaphore_signal(barrier, inc=1, device_id=partner, device_id_type=MESH)

    rows_y = ds(y * ROW_FEATS, ROW_FEATS, ROW_FEATS)
    cols_x = ds(x * FEATS, FEATS, 128)
    cols_y = ds(y * COLS, COLS, 128)
    loads = [
        (down, down_v), (up, up_v), (gates, gate_v),
        (tok, tok_g.at[:, cols_x]), (cot, cot_g.at[:, cols_y]),
        (weight.at[rows_y, :], wg.at[:, cols_y]),
    ]
    loads = [pltpu.make_async_copy(s, d, local_sem.at[i]) for i, (s, d) in enumerate(loads)]
    for load in loads[:2]:
        load.start()

    started = []
    names = {}

    def remote(name, src, dst, device):
        i = names.setdefault(name, len(names))
        copy = pltpu.make_async_remote_copy(
            src_ref=src, dst_ref=dst, send_sem=send_sem.at[i], recv_sem=recv_sem.at[i],
            device_id=device, device_id_type=MESH,
        )
        copy.start()
        started.append(copy)
        return copy

    pl.semaphore_wait(barrier, len(partners))

    my_rows = ds(z * FEATS + c * PIECE, PIECE, PIECE)
    w_in = {}
    for step in (2, 1, 3):
        first = ring(y, step) * ROW_FEATS + z * FEATS + c * PIECE
        w_in[step] = remote(
            ("w", step), weight.at[ds(first, PIECE, PIECE), :], wg.at[my_rows, cols_y], at_y(step)
        )

    def chunk(half, k):
        return pl.ds(half * HALF + k * CHUNK, CHUNK)

    def gather_own(name, way, half, src, dst, cols, at):
        return [
            remote((name, way, half, k), src.at[chunk(half, k), :], dst.at[chunk(half, k), cols], at(1 if way == 0 else -1))
            for k in range(CHUNKS)
        ]

    def gather_first(name, src, dst, cols, at):
        return [gather_own(name, way, way, src, dst, cols, at) for way in (0, 1)]

    def gather_second(name, src, dst, cols, at):
        return [gather_own(name, way, 1 - way, src, dst, cols, at) for way in (0, 1)]

    def gather_relay(name, first, dst, pos, width, at):
        copies = []
        for k in range(CHUNKS):
            for way in (0, 1):
                first[way][k].wait_recv()
                step = 1 if way == 0 else -1
                here = dst.at[chunk(way, k), ds(ring(pos, -step) * width, width, 128)]
                copies.append(remote((name, "r", way, k), here, here, at(step)))
        return copies

    tok_first = gather_first("tok", tok, tok_g, cols_x, at_x)
    tok_second = gather_second("tok", tok, tok_g, cols_x, at_x)
    cot_first = gather_first("cot", cot, cot_g, cols_y, at_y)

    for load in loads[2:]:
        load.start()

    loads[0].wait()
    loads[1].wait()

    def fill(g, carry):
        picks = [jnp.int32(0)] * CAP
        count = jnp.int32(0)
        for j in range(USED):
            local = store_row[expert[j, g]] - seq * STORED
            mine = (local >= 0) & (local < STORED)
            for k in range(CAP):
                picks[k] = jnp.where(mine & (count == k), local, picks[k])
            count = count + mine.astype(jnp.int32)
        for k in range(CAP):
            ad_send[g * CAP + k, :, :FEATS] = down_v[picks[k]]
            ad_send[g * CAP + k, :, FEATS:] = up_v[picks[k]]
        return carry

    lax.fori_loop(0, SEQ, fill, 0)
    mine_slots = pl.ds(seq * CAP, CAP)
    ad_in = []
    for step in range(1, SEQ):
        target = at_seq(step)
        ad_in.append(
            remote(("ad", step), ad_send.at[pl.ds(target[0] * CAP, CAP)], ad_recv.at[mine_slots], target)
        )
    for k in range(CAP):
        ad_recv[seq * CAP + k] = ad_send[seq * CAP + k]

    core_in = []

    def to_core(name, place):
        core_in.append((name[1], remote(name, place, place, other_core)))

    def z_place(zz, q, part=None):
        first = zz * FEATS + c * PIECE + (0 if part is None else part * PART)
        return wg.at[ds(first, PIECE if part is None else PART, PART), ds(q * COLS, COLS, 128)]

    def z_start(step):
        w_in[step].wait_recv()
        q = ring(y, -step)
        n = lambda k: ("z", step, k)
        out = {}
        for part in (0, 1):
            here = z_place(z, q, part)
            out["p", part] = remote(n(("p", part)), here, here, at_z(1))
            here = z_place(z, q, 1 - part)
            out["m", 1 - part] = remote(n(("m", 1 - part)), here, here, at_z(-1))
        to_core(("core", step, 0), z_place(z, q))
        return out

    def z_relay(step, out):
        q = ring(y, -step)
        out["p", 0].wait_recv()
        here = z_place(ring(z, -1), q, 0)
        out["r", 0] = remote(("z", step, "r0"), here, here, at_z(1))
        out["m", 1].wait_recv()
        here = z_place(ring(z, 1), q, 1)
        out["r", 1] = remote(("z", step, "r1"), here, here, at_z(-1))

    def z_near(step, out):
        q = ring(y, -step)
        out["p", 1].wait_recv()
        to_core(("core", step, 3), z_place(ring(z, -1), q))
        out["m", 0].wait_recv()
        to_core(("core", step, 1), z_place(ring(z, 1), q))

    def z_far(step, out):
        q = ring(y, -step)
        out["r", 0].wait_recv()
        out["r", 1].wait_recv()
        to_core(("core", step, 2), z_place(ring(z, 2), q))

    def core_wait(step):
        for s, copy in core_in:
            if s == step:
                copy.wait_recv()

    z2 = z_start(2)
    tok_relay = gather_relay("tok", tok_first, tok_g, x, FEATS, at_x)

    for copy in ad_in:
        copy.wait_recv()
    holders = []
    for j in range(USED):
        holder = store_row[expert[j, seq]] // STORED
        rank = jnp.int32(0)
        for earlier in holders:
            rank = rank + (earlier == holder).astype(jnp.int32)
        holders.append(holder)
        rows = ad_recv[holder * CAP + rank]
        dd[pl.ds(j * RANK, RANK), cols_x] = rows[:, :FEATS]
        uu[pl.ds(j * RANK, RANK), cols_y] = rows[:, FEATS:]
    low_rows = pl.ds(0, LOW)
    up_in = []
    down_in = []
    for step in (2, 1, 3):
        here = uu.at[low_rows, cols_y]
        up_in.append(remote(("up", step), here, here, at_y(step)))
        here = dd.at[low_rows, cols_x]
        down_in.append(remote(("down", step), here, here, at_x(step)))
    cot_second = gather_second("cot", cot, cot_g, cols_y, at_y)

    z_relay(2, z2)
    z3 = z_start(3)
    z1 = z_start(1)
    z_near(2, z2)
    z_far(2, z2)

    loads[2].wait()
    for j in range(USED):
        row = jnp.broadcast_to(gate_v[pl.ds(j, 1), :], (RANK, GROUP))
        gate_t[pl.ds(j * RANK, RANK), :] = row
        gate_t[pl.ds(LOW + j * RANK, RANK), :] = row
    gate[...] = gate_t[...].T
    first_half = lax.broadcasted_iota(jnp.int32, (GROUP, 2 * LOW), 1) < LOW

    def split_gated(value, out):
        gated = value * gate[...]
        high = gated.astype(BF16).astype(F32)
        out[...] = jnp.where(first_half, high, gated - high).astype(BF16)

    for copy in tok_second[0] + tok_second[1] + tok_relay:
        copy.wait_recv()
    loads[3].wait()
    cot_relay = gather_relay("cot", cot_first, cot_g, y, COLS, at_y)
    for copy in down_in + up_in:
        copy.wait_recv()
    dd[LOW:, :] = dd[:LOW, :]
    uu[LOW:, :] = uu[:LOW, :]
    split_gated(
        lax.dot_general(tok_g[...], dd[...], TRANSPOSED, preferred_element_type=F32), low_hl
    )

    def project(q):
        cols = ds(q * COLS, COLS, 128)
        return jnp.dot(tok_g[...], wg[:, cols], preferred_element_type=F32) + jnp.dot(
            low_hl[...], uu[:, cols], preferred_element_type=F32
        )

    def input_grad(q):
        feats = ds(q * FEATS, FEATS, FEATS)
        return lax.dot_general(
            cot_g[...], wg[feats, :], TRANSPOSED, preferred_element_type=F32
        ) + jnp.dot(
            back_hl[...], dd[:, ds(q * FEATS, FEATS, 128)], preferred_element_type=F32
        )

    def far_send(name, value, far, relay, at):
        far[...] = value.astype(BF16)
        return [
            [
                remote((name, "f", way, k), far.at[chunk(way, k), :], relay.at[way, pl.ds(k * CHUNK, CHUNK), :], at(1 if way == 0 else -1))
                for k in range(CHUNKS)
            ]
            for way in (0, 1)
        ]

    def near_send(name, value, way, out, keep, arrive, at):
        direct = 1 - way
        out[pl.ds(direct * HALF, HALF), :] = value[direct * HALF : (direct + 1) * HALF].astype(BF16)
        copies = [
            remote((name, "n", way, k), out.at[chunk(direct, k), :], arrive.at[way, chunk(direct, k), :], at(1 if way == 0 else -1))
            for k in range(CHUNKS)
        ]
        keep[way] = value[way * HALF : (way + 1) * HALF]
        return copies

    def relay_send(name, far_in, way, k, out, keep, relay, arrive, at):
        far_in[way][k].wait_recv()
        inner = pl.ds(k * CHUNK, CHUNK)
        outer = chunk(way, k)
        out[outer, :] = (keep[way, inner, :] + relay[way, inner, :].astype(F32)).astype(BF16)
        return remote((name, "s", way, k), out.at[outer, :], arrive.at[way, outer, :], at(1 if way == 0 else -1))

    def finish(near, sums, way, k, own, arrive, out, result, sem):
        near[1 - way][k].wait_recv()
        sums[way][k].wait_recv()
        rows = chunk(way, k)
        out[rows, :] = (
            own[rows, :] + arrive[0, rows, :].astype(F32) + arrive[1, rows, :].astype(F32)
        ).astype(BF16)
        copy = pltpu.make_async_copy(out.at[rows, :], result.at[rows, :], local_sem.at[sem])
        copy.start()
        return copy

    core_wait(2)
    loads[5].wait()
    y_far_in = far_send("y", project(ring(y, 2)), y_far, y_relay, at_y)
    z_relay(3, z3)
    y_own[...] = project(y)
    z_near(3, z3)
    z_relay(1, z1)
    z_near(1, z1)
    z_far(3, z3)
    z_far(1, z1)
    core_wait(3)
    core_wait(1)

    loads[4].wait()
    for copy in cot_second[0] + cot_second[1]:
        copy.wait_recv()
    x2_feats = ds(ring(x, 2) * FEATS, FEATS, FEATS)

    def back_of(q):
        cols = ds(q * COLS, COLS, 128)
        return lax.dot_general(cot_g[:, cols], uu[:, cols], TRANSPOSED, preferred_element_type=F32)

    def x2_of(q):
        cols = ds(q * COLS, COLS, 128)
        return lax.dot_general(cot_g[:, cols], wg[x2_feats, cols], TRANSPOSED, preferred_element_type=F32)

    back_part[...] = back_of(y) + back_of(ring(y, 1)) + back_of(ring(y, -1))
    x2_part[...] = x2_of(y) + x2_of(ring(y, 1)) + x2_of(ring(y, -1))

    y_near = [
        near_send("y", project(ring(y, 1)), 0, y_plus, y_keep, y_in, at_y),
        near_send("y", project(ring(y, -1)), 1, y_minus, y_keep, y_in, at_y),
    ]

    for copy in cot_relay:
        copy.wait_recv()
    split_gated(back_part[...] + back_of(ring(y, 2)), back_hl)
    x2_value = x2_part[...] + x2_of(ring(y, 2)) + jnp.dot(
        back_hl[...], dd[:, ds(ring(x, 2) * FEATS, FEATS, 128)], preferred_element_type=F32
    )
    x_far_in = far_send("x", x2_value, x_far, x_relay, at_x)
    x_near = [
        near_send("x", input_grad(ring(x, 1)), 0, x_plus, x_keep, x_in, at_x),
        near_send("x", input_grad(ring(x, -1)), 1, x_minus, x_keep, x_in, at_x),
    ]
    x_own[...] = input_grad(x)
    y_sums, x_sums = ([], []), ([], [])
    for k in range(CHUNKS):
        y_sums[0].append(relay_send("y", y_far_in, 0, k, y_plus, y_keep, y_relay, y_in, at_y))
        y_sums[1].append(relay_send("y", y_far_in, 1, k, y_minus, y_keep, y_relay, y_in, at_y))
        x_sums[0].append(relay_send("x", x_far_in, 0, k, x_plus, x_keep, x_relay, x_in, at_x))
        x_sums[1].append(relay_send("x", x_far_in, 1, k, x_minus, x_keep, x_relay, x_in, at_x))
    last = []
    for k in range(CHUNKS):
        for way in (0, 1):
            last.append(finish(x_near, x_sums, way, k, x_own, x_in, x_out, grad_tokens, len(loads) + len(last)))
        for way in (0, 1):
            last.append(finish(y_near, y_sums, way, k, y_own, y_in, y_out, projected, len(loads) + len(last)))
    for copy in last:
        copy.wait()
    for copy in started:
        copy.wait_send()


def copy_kernel(a, b, a_out, b_out, a_v, b_v, in_sems, out_sems):
    pairs = []
    for i, (src, held, dst) in enumerate(((a, a_v, a_out), (b, b_v, b_out))):
        for k in range(COPIES):
            rows = pl.ds(k * (GROUP // COPIES), GROUP // COPIES)
            pairs.append((
                pltpu.make_async_copy(src.at[rows, :], held.at[rows, :], in_sems.at[i, k]),
                pltpu.make_async_copy(held.at[rows, :], dst.at[rows, :], out_sems.at[i, k]),
            ))
    for fetch, _ in pairs:
        fetch.start()
    for fetch, store in pairs:
        fetch.wait()
        store.start()
    for _, store in pairs:
        store.wait()


def per_device(tokens, cotangent, gates, weight, down, up, expert, store_row):
    any_space = pl.BlockSpec(memory_space=pl.ANY)
    smem = pl.BlockSpec(memory_space=pltpu.SMEM)

    def ring_scratch(width):
        return [
            pltpu.VMEM((GROUP, width), BF16),
            pltpu.VMEM((GROUP, width), BF16),
            pltpu.VMEM((GROUP, width), BF16),
            pltpu.VMEM((2, HALF, width), F32),
            pltpu.VMEM((GROUP, width), F32),
            pltpu.VMEM((2, HALF, width), BF16),
            pltpu.VMEM((2, GROUP, width), BF16),
            pltpu.VMEM((GROUP, width), BF16),
        ]

    flops = 2 * 2 * GROUP * ROW_FEATS * ROW_COLS
    outs = (
        jax.ShapeDtypeStruct((GROUP, COLS), BF16),
        jax.ShapeDtypeStruct((GROUP, FEATS), BF16),
    )
    result = pl.pallas_call(
        kernel,
        out_shape=outs,
        in_specs=[any_space] * 6 + [smem] * 2,
        out_specs=(any_space, any_space),
        scratch_shapes=[
            pltpu.VMEM((ROW_FEATS, ROW_COLS), BF16),
            pltpu.VMEM((GROUP, ROW_FEATS), BF16),
            pltpu.VMEM((GROUP, ROW_COLS), BF16),
            pltpu.VMEM((USED, GROUP), F32),
            pltpu.VMEM((2 * LOW, GROUP), F32),
            pltpu.VMEM((GROUP, 2 * LOW), F32),
            pltpu.VMEM((STORED, RANK, FEATS), BF16),
            pltpu.VMEM((STORED, RANK, COLS), BF16),
            pltpu.VMEM((SEQ * CAP, RANK, FEATS + COLS), BF16),
            pltpu.VMEM((SEQ * CAP, RANK, FEATS + COLS), BF16),
            pltpu.VMEM((2 * LOW, ROW_FEATS), BF16),
            pltpu.VMEM((2 * LOW, ROW_COLS), BF16),
            pltpu.VMEM((GROUP, 2 * LOW), BF16),
            pltpu.VMEM((GROUP, 2 * LOW), BF16),
            pltpu.VMEM((GROUP, 2 * LOW), F32),
            pltpu.VMEM((GROUP, FEATS), F32),
        ]
        + ring_scratch(COLS)
        + ring_scratch(FEATS)
        + [
            pltpu.SemaphoreType.DMA((6 + 4 * CHUNKS,)),
            pltpu.SemaphoreType.DMA((N_SEMS,)),
            pltpu.SemaphoreType.DMA((N_SEMS,)),
        ],
        compiler_params=pltpu.CompilerParams(
            collective_id=0, has_side_effects=True, vmem_limit_bytes=60 * 2**20
        ),
        cost_estimate=pl.CostEstimate(flops=flops, bytes_accessed=20 * 2**20, transcendentals=0),
        name="mixture",
    )(tokens, cotangent, gates.T, weight, down, up, expert.T, store_row)
    return pl.pallas_call(
        copy_kernel,
        out_shape=outs,
        in_specs=[any_space] * 2,
        out_specs=(any_space, any_space),
        scratch_shapes=[
            pltpu.VMEM((GROUP, COLS), BF16),
            pltpu.VMEM((GROUP, FEATS), BF16),
            pltpu.SemaphoreType.DMA((2, COPIES)),
            pltpu.SemaphoreType.DMA((2, COPIES)),
        ],
        compiler_params=pltpu.CompilerParams(vmem_limit_bytes=60 * 2**20),
        name="results",
    )(*result)


def solution(mesh):
    return jax.shard_map(
        per_device,
        mesh=mesh,
        in_specs=(
            P("seq", "tensor"),
            P("seq", "tensor"),
            P("seq", None),
            P(None, "tensor"),
            P("seq", None, "tensor"),
            P("seq", None, "tensor"),
            P(),
            P(),
        ),
        out_specs=(P("seq", "tensor"), P("seq", "tensor")),
        check_vma=False,
    )
```

```python
import jax
import jax.numpy as jnp
from jax import lax
from jax.experimental import pallas as pl
from jax.experimental.pallas import tpu as pltpu
from jax.sharding import PartitionSpec as P

F32 = jnp.float32
BF16 = jnp.bfloat16
MESH = pl.DeviceIdType.MESH
RING = 4
CORES = 2
GROUP = 768
HALF = GROUP // 2
FEATS = 512
COLS = 640
ROW_FEATS = RING * FEATS
ROW_COLS = RING * COLS
RANK = 16
USED = 4
LOW = USED * RANK
STORED = 128
SEQ = RING * CORES
CAP = 2
PIECE = FEATS // CORES
PART = PIECE // 2
CHUNKS = 3
CHUNK = HALF // CHUNKS
TRANSPOSED = (((1,), (1,)), ((), ()))
N_SEMS = 128
COPIES = 4


def ds(start, size, align):
    return pl.ds(pl.multiple_of(start, align), size)


def kernel(
    tok, cot, gates, weight, down, up, expert_in, store_row_in,
    projected, grad_tokens,
    wg, tok_g, cot_g, gate_v, gate_t, gate, down_v, up_v, ad_send, ad_recv, dd, uu, low_hl, back_hl,
    back_part, x2_part,
    y_far, y_plus, y_minus, y_keep, y_own, y_relay, y_in, y_out,
    x_far, x_plus, x_minus, x_keep, x_own, x_relay, x_in, x_out,
    expert, store_row, local_sem, send_sem, recv_sem,
):
    seq, ten = lax.axis_index("seq"), lax.axis_index("tensor")
    z, c = seq // CORES, lax.rem(seq, CORES)
    y, x = ten // RING, lax.rem(ten, RING)

    def ring(value, step):
        return lax.rem(value + (step + RING), RING)

    def at_x(step):
        return (seq, y * RING + ring(x, step))

    def at_y(step):
        return (seq, ring(y, step) * RING + x)

    def at_z(step):
        return (ring(z, step) * CORES + c, ten)

    other_core = (z * CORES + (1 - c), ten)

    def at_seq(step):
        return (lax.rem(seq + step, SEQ), ten)

    barrier = pltpu.get_barrier_semaphore()
    partners = [at_x(s) for s in (1, 2, 3)] + [at_y(s) for s in (1, 2, 3)]
    partners += [at_seq(s) for s in range(1, SEQ)]
    for partner in partners:
        pl.semaphore_signal(barrier, inc=1, device_id=partner, device_id_type=MESH)

    rows_y = ds(y * ROW_FEATS, ROW_FEATS, ROW_FEATS)
    cols_x = ds(x * FEATS, FEATS, 128)
    cols_y = ds(y * COLS, COLS, 128)
    loads = [
        (down, down_v), (up, up_v), (gates, gate_v),
        (tok, tok_g.at[:, cols_x]), (cot, cot_g.at[:, cols_y]),
        (weight.at[rows_y, :], wg.at[:, cols_y]), (expert_in, expert), (store_row_in, store_row),
    ]
    loads = [pltpu.make_async_copy(s, d, local_sem.at[i]) for i, (s, d) in enumerate(loads)]
    for load in loads[6:] + loads[:2]:
        load.start()

    started = []
    names = {}

    def remote(name, src, dst, device):
        i = names.setdefault(name, len(names))
        copy = pltpu.make_async_remote_copy(
            src_ref=src, dst_ref=dst, send_sem=send_sem.at[i], recv_sem=recv_sem.at[i],
            device_id=device, device_id_type=MESH,
        )
        copy.start()
        started.append(copy)
        return copy

    pl.semaphore_wait(barrier, len(partners))

    my_rows = ds(z * FEATS + c * PIECE, PIECE, PIECE)
    w_in = {}
    for step in (2, 1, 3):
        first = ring(y, step) * ROW_FEATS + z * FEATS + c * PIECE
        w_in[step] = remote(
            ("w", step), weight.at[ds(first, PIECE, PIECE), :], wg.at[my_rows, cols_y], at_y(step)
        )

    def chunk(half, k):
        return pl.ds(half * HALF + k * CHUNK, CHUNK)

    def gather_own(name, way, half, src, dst, cols, at):
        return [
            remote((name, way, half, k), src.at[chunk(half, k), :], dst.at[chunk(half, k), cols], at(1 if way == 0 else -1))
            for k in range(CHUNKS)
        ]

    def gather_first(name, src, dst, cols, at):
        return [gather_own(name, way, way, src, dst, cols, at) for way in (0, 1)]

    def gather_second(name, src, dst, cols, at):
        return [gather_own(name, way, 1 - way, src, dst, cols, at) for way in (0, 1)]

    def gather_relay(name, first, dst, pos, width, at):
        copies = []
        for k in range(CHUNKS):
            for way in (0, 1):
                first[way][k].wait_recv()
                step = 1 if way == 0 else -1
                here = dst.at[chunk(way, k), ds(ring(pos, -step) * width, width, 128)]
                copies.append(remote((name, "r", way, k), here, here, at(step)))
        return copies

    tok_first = gather_first("tok", tok, tok_g, cols_x, at_x)
    tok_second = gather_second("tok", tok, tok_g, cols_x, at_x)
    cot_first = gather_first("cot", cot, cot_g, cols_y, at_y)

    for load in loads[2:6]:
        load.start()

    for load in loads[6:] + loads[:2]:
        load.wait()

    def fill(g, carry):
        picks = [jnp.int32(0)] * CAP
        count = jnp.int32(0)
        for j in range(USED):
            local = store_row[expert[j, g]] - seq * STORED
            mine = (local >= 0) & (local < STORED)
            for k in range(CAP):
                picks[k] = jnp.where(mine & (count == k), local, picks[k])
            count = count + mine.astype(jnp.int32)
        for k in range(CAP):
            ad_send[g * CAP + k, :, :FEATS] = down_v[picks[k]]
            ad_send[g * CAP + k, :, FEATS:] = up_v[picks[k]]
        return carry

    lax.fori_loop(0, SEQ, fill, 0)
    mine_slots = pl.ds(seq * CAP, CAP)
    ad_in = []
    for step in range(1, SEQ):
        target = at_seq(step)
        ad_in.append(
            remote(("ad", step), ad_send.at[pl.ds(target[0] * CAP, CAP)], ad_recv.at[mine_slots], target)
        )
    for k in range(CAP):
        ad_recv[seq * CAP + k] = ad_send[seq * CAP + k]

    core_in = []

    def to_core(name, place):
        core_in.append((name[1], remote(name, place, place, other_core)))

    def z_place(zz, q, part=None):
        first = zz * FEATS + c * PIECE + (0 if part is None else part * PART)
        return wg.at[ds(first, PIECE if part is None else PART, PART), ds(q * COLS, COLS, 128)]

    def z_start(step):
        w_in[step].wait_recv()
        q = ring(y, -step)
        n = lambda k: ("z", step, k)
        out = {}
        for part in (0, 1):
            here = z_place(z, q, part)
            out["p", part] = remote(n(("p", part)), here, here, at_z(1))
            here = z_place(z, q, 1 - part)
            out["m", 1 - part] = remote(n(("m", 1 - part)), here, here, at_z(-1))
        to_core(("core", step, 0), z_place(z, q))
        return out

    def z_relay(step, out):
        q = ring(y, -step)
        out["p", 0].wait_recv()
        here = z_place(ring(z, -1), q, 0)
        out["r", 0] = remote(("z", step, "r0"), here, here, at_z(1))
        out["m", 1].wait_recv()
        here = z_place(ring(z, 1), q, 1)
        out["r", 1] = remote(("z", step, "r1"), here, here, at_z(-1))

    def z_near(step, out):
        q = ring(y, -step)
        out["p", 1].wait_recv()
        to_core(("core", step, 3), z_place(ring(z, -1), q))
        out["m", 0].wait_recv()
        to_core(("core", step, 1), z_place(ring(z, 1), q))

    def z_far(step, out):
        q = ring(y, -step)
        out["r", 0].wait_recv()
        out["r", 1].wait_recv()
        to_core(("core", step, 2), z_place(ring(z, 2), q))

    def core_wait(step):
        for s, copy in core_in:
            if s == step:
                copy.wait_recv()

    z2 = z_start(2)
    tok_relay = gather_relay("tok", tok_first, tok_g, x, FEATS, at_x)

    for copy in ad_in:
        copy.wait_recv()
    holders = []
    for j in range(USED):
        holder = store_row[expert[j, seq]] // STORED
        rank = jnp.int32(0)
        for earlier in holders:
            rank = rank + (earlier == holder).astype(jnp.int32)
        holders.append(holder)
        rows = ad_recv[holder * CAP + rank]
        dd[pl.ds(j * RANK, RANK), cols_x] = rows[:, :FEATS]
        uu[pl.ds(j * RANK, RANK), cols_y] = rows[:, FEATS:]
    low_rows = pl.ds(0, LOW)
    up_in = []
    down_in = []
    for step in (2, 1, 3):
        here = uu.at[low_rows, cols_y]
        up_in.append(remote(("up", step), here, here, at_y(step)))
        here = dd.at[low_rows, cols_x]
        down_in.append(remote(("down", step), here, here, at_x(step)))
    cot_second = gather_second("cot", cot, cot_g, cols_y, at_y)

    z_relay(2, z2)
    z3 = z_start(3)
    z1 = z_start(1)
    z_near(2, z2)
    z_far(2, z2)

    loads[2].wait()
    for j in range(USED):
        row = jnp.broadcast_to(gate_v[pl.ds(j, 1), :], (RANK, GROUP))
        gate_t[pl.ds(j * RANK, RANK), :] = row
        gate_t[pl.ds(LOW + j * RANK, RANK), :] = row
    gate[...] = gate_t[...].T
    first_half = lax.broadcasted_iota(jnp.int32, (GROUP, 2 * LOW), 1) < LOW

    def split_gated(value, out):
        gated = value * gate[...]
        high = gated.astype(BF16).astype(F32)
        out[...] = jnp.where(first_half, high, gated - high).astype(BF16)

    for copy in tok_second[0] + tok_second[1] + tok_relay:
        copy.wait_recv()
    loads[3].wait()
    cot_relay = gather_relay("cot", cot_first, cot_g, y, COLS, at_y)
    for copy in down_in + up_in:
        copy.wait_recv()
    dd[LOW:, :] = dd[:LOW, :]
    uu[LOW:, :] = uu[:LOW, :]
    split_gated(
        lax.dot_general(tok_g[...], dd[...], TRANSPOSED, preferred_element_type=F32), low_hl
    )

    def project(q):
        cols = ds(q * COLS, COLS, 128)
        return jnp.dot(tok_g[...], wg[:, cols], preferred_element_type=F32) + jnp.dot(
            low_hl[...], uu[:, cols], preferred_element_type=F32
        )

    def input_grad(q):
        feats = ds(q * FEATS, FEATS, FEATS)
        return lax.dot_general(
            cot_g[...], wg[feats, :], TRANSPOSED, preferred_element_type=F32
        ) + jnp.dot(
            back_hl[...], dd[:, ds(q * FEATS, FEATS, 128)], preferred_element_type=F32
        )

    def far_send(name, value, far, relay, at):
        far[...] = value.astype(BF16)
        return [
            [
                remote((name, "f", way, k), far.at[chunk(way, k), :], relay.at[way, pl.ds(k * CHUNK, CHUNK), :], at(1 if way == 0 else -1))
                for k in range(CHUNKS)
            ]
            for way in (0, 1)
        ]

    def near_compute(value, way, out, keep):
        direct = 1 - way
        out[pl.ds(direct * HALF, HALF), :] = value[direct * HALF : (direct + 1) * HALF].astype(BF16)
        keep[way] = value[way * HALF : (way + 1) * HALF]

    def near_send(name, way, out, arrive, at):
        rows = [chunk(1 - way, k) for k in range(CHUNKS)]
        return [
            remote((name, "n", way, k), out.at[rows[k], :], arrive.at[way, rows[k], :], at(1 if way == 0 else -1))
            for k in range(CHUNKS)
        ]

    def relay_send(name, far_in, way, k, out, keep, relay, arrive, at):
        far_in[way][k].wait_recv()
        inner = pl.ds(k * CHUNK, CHUNK)
        outer = chunk(way, k)
        out[outer, :] = (keep[way, inner, :] + relay[way, inner, :].astype(F32)).astype(BF16)
        return remote((name, "s", way, k), out.at[outer, :], arrive.at[way, outer, :], at(1 if way == 0 else -1))

    def finish(near, sums, way, k, own, arrive, out, result, sem):
        near[1 - way][k].wait_recv()
        sums[way][k].wait_recv()
        rows = chunk(way, k)
        out[rows, :] = (
            own[rows, :] + arrive[0, rows, :].astype(F32) + arrive[1, rows, :].astype(F32)
        ).astype(BF16)
        copy = pltpu.make_async_copy(out.at[rows, :], result.at[rows, :], local_sem.at[sem])
        copy.start()
        return copy

    x2_feats = ds(ring(x, 2) * FEATS, FEATS, FEATS)

    def back_of(q):
        cols = ds(q * COLS, COLS, 128)
        return lax.dot_general(cot_g[:, cols], uu[:, cols], TRANSPOSED, preferred_element_type=F32)

    def x2_of(q):
        cols = ds(q * COLS, COLS, 128)
        return lax.dot_general(cot_g[:, cols], wg[x2_feats, cols], TRANSPOSED, preferred_element_type=F32)

    core_wait(2)
    loads[5].wait()
    y_far_in = far_send("y", project(ring(y, 2)), y_far, y_relay, at_y)
    z_relay(3, z3)
    y_own[...] = project(y)
    z_near(3, z3)
    z_relay(1, z1)
    loads[4].wait()
    x2_part[...] = x2_of(y)
    z_far(3, z3)
    z_near(1, z1)
    z_far(1, z1)
    core_wait(3)
    for copy in cot_second[0] + cot_second[1]:
        copy.wait_recv()
    back_part[...] = back_of(y) + back_of(ring(y, 1)) + back_of(ring(y, -1))
    x2_part[...] += x2_of(ring(y, 1))
    core_wait(1)
    x2_part[...] += x2_of(ring(y, -1))
    near_compute(project(ring(y, 1)), 0, y_plus, y_keep)

    for copy in cot_relay:
        copy.wait_recv()
    split_gated(back_part[...] + back_of(ring(y, 2)), back_hl)
    x2_value = x2_part[...] + x2_of(ring(y, 2)) + jnp.dot(
        back_hl[...], dd[:, ds(ring(x, 2) * FEATS, FEATS, 128)], preferred_element_type=F32
    )
    x_far_in = far_send("x", x2_value, x_far, x_relay, at_x)
    y_near = [near_send("y", 0, y_plus, y_in, at_y)]
    near_compute(project(ring(y, -1)), 1, y_minus, y_keep)
    y_near.append(near_send("y", 1, y_minus, y_in, at_y))
    near_compute(input_grad(ring(x, 1)), 0, x_plus, x_keep)
    x_near = [near_send("x", 0, x_plus, x_in, at_x)]
    near_compute(input_grad(ring(x, -1)), 1, x_minus, x_keep)
    x_near.append(near_send("x", 1, x_minus, x_in, at_x))
    x_own[...] = input_grad(x)
    y_sums, x_sums = ([], []), ([], [])
    for k in range(CHUNKS):
        y_sums[0].append(relay_send("y", y_far_in, 0, k, y_plus, y_keep, y_relay, y_in, at_y))
        y_sums[1].append(relay_send("y", y_far_in, 1, k, y_minus, y_keep, y_relay, y_in, at_y))
        x_sums[0].append(relay_send("x", x_far_in, 0, k, x_plus, x_keep, x_relay, x_in, at_x))
        x_sums[1].append(relay_send("x", x_far_in, 1, k, x_minus, x_keep, x_relay, x_in, at_x))
    last = []
    for k in range(CHUNKS):
        for way in (0, 1):
            last.append(finish(x_near, x_sums, way, k, x_own, x_in, x_out, grad_tokens, len(loads) + len(last)))
        for way in (0, 1):
            last.append(finish(y_near, y_sums, way, k, y_own, y_in, y_out, projected, len(loads) + len(last)))
    for copy in last:
        copy.wait()
    for copy in started:
        copy.wait_send()


def copy_kernel(a, b, a_out, b_out, a_v, b_v, in_sems, out_sems):
    pairs = []
    for i, (src, held, dst) in enumerate(((a, a_v, a_out), (b, b_v, b_out))):
        for k in range(COPIES):
            rows = pl.ds(k * (GROUP // COPIES), GROUP // COPIES)
            pairs.append((
                pltpu.make_async_copy(src.at[rows, :], held.at[rows, :], in_sems.at[i, k]),
                pltpu.make_async_copy(held.at[rows, :], dst.at[rows, :], out_sems.at[i, k]),
            ))
    for fetch, _ in pairs:
        fetch.start()
    for fetch, store in pairs:
        fetch.wait()
        store.start()
    for _, store in pairs:
        store.wait()


def per_device(tokens, cotangent, gates, weight, down, up, expert, store_row):
    any_space = pl.BlockSpec(memory_space=pl.ANY)

    def ring_scratch(width):
        return [
            pltpu.VMEM((GROUP, width), BF16),
            pltpu.VMEM((GROUP, width), BF16),
            pltpu.VMEM((GROUP, width), BF16),
            pltpu.VMEM((2, HALF, width), F32),
            pltpu.VMEM((GROUP, width), F32),
            pltpu.VMEM((2, HALF, width), BF16),
            pltpu.VMEM((2, GROUP, width), BF16),
            pltpu.VMEM((GROUP, width), BF16),
        ]

    flops = 2 * 2 * GROUP * ROW_FEATS * ROW_COLS
    outs = (
        jax.ShapeDtypeStruct((GROUP, COLS), BF16),
        jax.ShapeDtypeStruct((GROUP, FEATS), BF16),
    )
    result = pl.pallas_call(
        kernel,
        out_shape=outs,
        in_specs=[any_space] * 8,
        out_specs=(any_space, any_space),
        scratch_shapes=[
            pltpu.VMEM((ROW_FEATS, ROW_COLS), BF16),
            pltpu.VMEM((GROUP, ROW_FEATS), BF16),
            pltpu.VMEM((GROUP, ROW_COLS), BF16),
            pltpu.VMEM((USED, GROUP), F32),
            pltpu.VMEM((2 * LOW, GROUP), F32),
            pltpu.VMEM((GROUP, 2 * LOW), F32),
            pltpu.VMEM((STORED, RANK, FEATS), BF16),
            pltpu.VMEM((STORED, RANK, COLS), BF16),
            pltpu.VMEM((SEQ * CAP, RANK, FEATS + COLS), BF16),
            pltpu.VMEM((SEQ * CAP, RANK, FEATS + COLS), BF16),
            pltpu.VMEM((2 * LOW, ROW_FEATS), BF16),
            pltpu.VMEM((2 * LOW, ROW_COLS), BF16),
            pltpu.VMEM((GROUP, 2 * LOW), BF16),
            pltpu.VMEM((GROUP, 2 * LOW), BF16),
            pltpu.VMEM((GROUP, 2 * LOW), F32),
            pltpu.VMEM((GROUP, FEATS), F32),
        ]
        + ring_scratch(COLS)
        + ring_scratch(FEATS)
        + [
            pltpu.SMEM((USED, SEQ), jnp.int32),
            pltpu.SMEM((SEQ * STORED,), jnp.int32),
            pltpu.SemaphoreType.DMA((8 + 4 * CHUNKS,)),
            pltpu.SemaphoreType.DMA((N_SEMS,)),
            pltpu.SemaphoreType.DMA((N_SEMS,)),
        ],
        compiler_params=pltpu.CompilerParams(
            collective_id=0, has_side_effects=True, vmem_limit_bytes=60 * 2**20
        ),
        cost_estimate=pl.CostEstimate(flops=flops, bytes_accessed=20 * 2**20, transcendentals=0),
        name="mixture",
    )(tokens, cotangent, gates.T, weight, down, up, expert.T, store_row)
    return pl.pallas_call(
        copy_kernel,
        out_shape=outs,
        in_specs=[any_space] * 2,
        out_specs=(any_space, any_space),
        scratch_shapes=[
            pltpu.VMEM((GROUP, COLS), BF16),
            pltpu.VMEM((GROUP, FEATS), BF16),
            pltpu.SemaphoreType.DMA((2, COPIES)),
            pltpu.SemaphoreType.DMA((2, COPIES)),
        ],
        compiler_params=pltpu.CompilerParams(vmem_limit_bytes=60 * 2**20),
        name="results",
    )(*result)


def solution(mesh):
    return jax.shard_map(
        per_device,
        mesh=mesh,
        in_specs=(
            P("seq", "tensor"),
            P("seq", "tensor"),
            P("seq", None),
            P(None, "tensor"),
            P("seq", None, "tensor"),
            P("seq", None, "tensor"),
            P(),
            P(),
        ),
        out_specs=(P("seq", "tensor"), P("seq", "tensor")),
        check_vma=False,
    )
```

```python
import math

import jax
import jax.numpy as jnp
from jax import lax
from jax.experimental import pallas as pl
from jax.experimental.pallas import tpu as pltpu
from jax.sharding import PartitionSpec as P

F32 = jnp.float32
BF16 = jnp.bfloat16
MESH = pl.DeviceIdType.MESH
RING = 4
CORES = 2
GROUP = 768
HALF = GROUP // 2
FEATS = 512
COLS = 640
ROW_FEATS = RING * FEATS
ROW_COLS = RING * COLS
RANK = 16
USED = 4
LOW = USED * RANK
STORED = 128
SEQ = RING * CORES
CAP = 2
PIECE = FEATS // CORES
PART = PIECE // 2
CHUNKS = 3
CHUNK = HALF // CHUNKS
TRANSPOSED = (((1,), (1,)), ((), ()))
N_SEND = 10
N_RECV = 79
COPIES = 2


def ds(start, size, align):
    return pl.ds(pl.multiple_of(start, align), size)


def kernel(
    tok, cot, gates, weight, down, up, expert_in, store_row_in,
    projected, grad_tokens,
    wg, tok_g, cot_g, gate_v, gate_t, gate, down_v, up_v, ad_send, ad_recv, dd, uu, low_hl, back_hl,
    back_part, x2_part,
    y_far, y_plus, y_minus, y_keep, y_own, y_relay, y_in, y_out,
    x_far, x_plus, x_minus, x_keep, x_own, x_relay, x_in, x_out,
    expert, store_row, local_sem, send_sem, recv_sem,
):
    seq, ten = lax.axis_index("seq"), lax.axis_index("tensor")
    z, c = seq // CORES, lax.rem(seq, CORES)
    y, x = ten // RING, lax.rem(ten, RING)

    def ring(value, step):
        return lax.rem(value + (step + RING), RING)

    def at_x(step):
        return (seq, y * RING + ring(x, step))

    def at_y(step):
        return (seq, ring(y, step) * RING + x)

    def at_z(step):
        return (ring(z, step) * CORES + c, ten)

    other_core = (z * CORES + (1 - c), ten)

    def at_seq(step):
        return (lax.rem(seq + step, SEQ), ten)

    barrier = pltpu.get_barrier_semaphore()
    partners = [at_x(s) for s in (1, 2, 3)] + [at_y(s) for s in (1, 2, 3)]
    partners += [at_seq(s) for s in range(1, SEQ)]
    for partner in partners:
        pl.semaphore_signal(barrier, inc=1, device_id=partner, device_id_type=MESH)

    rows_y = ds(y * ROW_FEATS, ROW_FEATS, ROW_FEATS)
    cols_x = ds(x * FEATS, FEATS, 128)
    cols_y = ds(y * COLS, COLS, 128)
    loads = [
        (down, down_v), (up, up_v), (gates, gate_v),
        (tok, tok_g.at[:, cols_x]), (cot, cot_g.at[:, cols_y]),
        (weight.at[rows_y, :], wg.at[:, cols_y]), (expert_in, expert), (store_row_in, store_row),
    ]
    loads = [pltpu.make_async_copy(s, d, local_sem.at[i]) for i, (s, d) in enumerate(loads)]
    for load in loads[6:] + loads[:2]:
        load.start()

    send_index, recv_index, sent, received = {}, {}, {}, {}

    def remote(name, src, dst, device, together=None):
        kind, key = name[0], name if together is None else together
        copy = pltpu.make_async_remote_copy(
            src_ref=src,
            dst_ref=dst,
            send_sem=send_sem.at[send_index.setdefault(kind, len(send_index))],
            recv_sem=recv_sem.at[recv_index.setdefault(key, len(recv_index))],
            device_id=device,
            device_id_type=MESH,
        )
        copy.start()
        size = math.prod(src.shape)
        sent[kind] = sent.get(kind, 0) + size
        received[key] = received.get(key, 0) + size
        return copy

    def wait_for(kind, size, sem):
        if kind == "ad":
            whole = ad_send.at[pl.ds(0, size // math.prod(ad_send.shape[1:]))]
        else:
            array = tok_g if kind in ("tok", "x", "down") else wg
            whole = array.at[pl.ds(0, size // array.shape[1]), :]
        pltpu.make_async_copy(whole, whole, sem).wait()

    def arrived(key):
        wait_for(key[0], received[key], recv_sem.at[recv_index[key]])

    pl.semaphore_wait(barrier, len(partners))

    my_rows = ds(z * FEATS + c * PIECE, PIECE, PIECE)
    w_in = {}
    for step in (2, 1, 3):
        first = ring(y, step) * ROW_FEATS + z * FEATS + c * PIECE
        w_in[step] = remote(
            ("w", step), weight.at[ds(first, PIECE, PIECE), :], wg.at[my_rows, cols_y], at_y(step)
        )

    def chunk(half, k):
        return pl.ds(half * HALF + k * CHUNK, CHUNK)

    def gather_own(name, way, half, src, dst, cols, at, together=None):
        return [
            remote((name, way, half, k), src.at[chunk(half, k), :], dst.at[chunk(half, k), cols], at(1 if way == 0 else -1), together)
            for k in range(CHUNKS)
        ]

    def gather_first(name, src, dst, cols, at):
        return [gather_own(name, way, way, src, dst, cols, at) for way in (0, 1)]

    def gather_second(name, src, dst, cols, at):
        for way in (0, 1):
            gather_own(name, way, 1 - way, src, dst, cols, at, (name, "second"))

    def gather_relay(name, first, dst, pos, width, at):
        for k in range(CHUNKS):
            for way in (0, 1):
                first[way][k].wait_recv()
                step = 1 if way == 0 else -1
                here = dst.at[chunk(way, k), ds(ring(pos, -step) * width, width, 128)]
                remote((name, "r", way, k), here, here, at(step), (name, "relay"))

    tok_first = gather_first("tok", tok, tok_g, cols_x, at_x)
    gather_second("tok", tok, tok_g, cols_x, at_x)
    cot_first = gather_first("cot", cot, cot_g, cols_y, at_y)

    for load in loads[2:6]:
        load.start()

    for load in loads[6:] + loads[:2]:
        load.wait()

    def fill(g, carry):
        picks = [jnp.int32(0)] * CAP
        count = jnp.int32(0)
        for j in range(USED):
            local = store_row[expert[j, g]] - seq * STORED
            mine = (local >= 0) & (local < STORED)
            for k in range(CAP):
                picks[k] = jnp.where(mine & (count == k), local, picks[k])
            count = count + mine.astype(jnp.int32)
        for k in range(CAP):
            ad_send[g * CAP + k, :, :FEATS] = down_v[picks[k]]
            ad_send[g * CAP + k, :, FEATS:] = up_v[picks[k]]
        return carry

    lax.fori_loop(0, SEQ, fill, 0)
    mine_slots = pl.ds(seq * CAP, CAP)
    for step in range(1, SEQ):
        target = at_seq(step)
        remote(("ad",), ad_send.at[pl.ds(target[0] * CAP, CAP)], ad_recv.at[mine_slots], target)
    for k in range(CAP):
        ad_recv[seq * CAP + k] = ad_send[seq * CAP + k]

    def to_core(step, place):
        remote(("core", step), place, place, other_core)

    def z_place(zz, q, part=None):
        first = zz * FEATS + c * PIECE + (0 if part is None else part * PART)
        return wg.at[ds(first, PIECE if part is None else PART, PART), ds(q * COLS, COLS, 128)]

    def z_start(step):
        w_in[step].wait_recv()
        q = ring(y, -step)
        n = lambda k: ("z", step, k)
        out = {}
        for part in (0, 1):
            here = z_place(z, q, part)
            out["p", part] = remote(n(("p", part)), here, here, at_z(1))
            here = z_place(z, q, 1 - part)
            out["m", 1 - part] = remote(n(("m", 1 - part)), here, here, at_z(-1))
        to_core(step, z_place(z, q))
        return out

    def z_relay(step, out):
        q = ring(y, -step)
        out["p", 0].wait_recv()
        here = z_place(ring(z, -1), q, 0)
        out["r", 0] = remote(("z", step, "r0"), here, here, at_z(1))
        out["m", 1].wait_recv()
        here = z_place(ring(z, 1), q, 1)
        out["r", 1] = remote(("z", step, "r1"), here, here, at_z(-1))

    def z_near(step, out):
        q = ring(y, -step)
        out["p", 1].wait_recv()
        to_core(step, z_place(ring(z, -1), q))
        out["m", 0].wait_recv()
        to_core(step, z_place(ring(z, 1), q))

    def z_far(step, out):
        q = ring(y, -step)
        out["r", 0].wait_recv()
        out["r", 1].wait_recv()
        to_core(step, z_place(ring(z, 2), q))

    def core_wait(step):
        arrived(("core", step))

    z2 = z_start(2)
    gather_relay("tok", tok_first, tok_g, x, FEATS, at_x)

    arrived(("ad",))
    holders = []
    for j in range(USED):
        holder = store_row[expert[j, seq]] // STORED
        rank = jnp.int32(0)
        for earlier in holders:
            rank = rank + (earlier == holder).astype(jnp.int32)
        holders.append(holder)
        rows = ad_recv[holder * CAP + rank]
        dd[pl.ds(j * RANK, RANK), cols_x] = rows[:, :FEATS]
        uu[pl.ds(j * RANK, RANK), cols_y] = rows[:, FEATS:]
    low_rows = pl.ds(0, LOW)
    for step in (2, 1, 3):
        here = uu.at[low_rows, cols_y]
        remote(("up",), here, here, at_y(step))
        here = dd.at[low_rows, cols_x]
        remote(("down",), here, here, at_x(step))
    gather_second("cot", cot, cot_g, cols_y, at_y)

    z_relay(2, z2)
    z3 = z_start(3)
    z1 = z_start(1)
    z_near(2, z2)
    z_far(2, z2)

    loads[2].wait()
    for j in range(USED):
        row = jnp.broadcast_to(gate_v[pl.ds(j, 1), :], (RANK, GROUP))
        gate_t[pl.ds(j * RANK, RANK), :] = row
        gate_t[pl.ds(LOW + j * RANK, RANK), :] = row
    gate[...] = gate_t[...].T
    first_half = lax.broadcasted_iota(jnp.int32, (GROUP, 2 * LOW), 1) < LOW

    def split_gated(value, out):
        gated = value * gate[...]
        high = gated.astype(BF16).astype(F32)
        out[...] = jnp.where(first_half, high, gated - high).astype(BF16)

    arrived(("tok", "second"))
    arrived(("tok", "relay"))
    loads[3].wait()
    gather_relay("cot", cot_first, cot_g, y, COLS, at_y)
    arrived(("down",))
    arrived(("up",))
    dd[LOW:, :] = dd[:LOW, :]
    uu[LOW:, :] = uu[:LOW, :]
    split_gated(
        lax.dot_general(tok_g[...], dd[...], TRANSPOSED, preferred_element_type=F32), low_hl
    )

    def project(q):
        cols = ds(q * COLS, COLS, 128)
        return jnp.dot(tok_g[...], wg[:, cols], preferred_element_type=F32) + jnp.dot(
            low_hl[...], uu[:, cols], preferred_element_type=F32
        )

    def input_grad(q):
        feats = ds(q * FEATS, FEATS, FEATS)
        return lax.dot_general(
            cot_g[...], wg[feats, :], TRANSPOSED, preferred_element_type=F32
        ) + jnp.dot(
            back_hl[...], dd[:, ds(q * FEATS, FEATS, 128)], preferred_element_type=F32
        )

    def far_send(name, value, far, relay, at):
        far[...] = value.astype(BF16)
        return [
            [
                remote((name, "f", way, k), far.at[chunk(way, k), :], relay.at[way, pl.ds(k * CHUNK, CHUNK), :], at(1 if way == 0 else -1))
                for k in range(CHUNKS)
            ]
            for way in (0, 1)
        ]

    def near_compute(value, way, out, keep):
        direct = 1 - way
        out[pl.ds(direct * HALF, HALF), :] = value[direct * HALF : (direct + 1) * HALF].astype(BF16)
        keep[way] = value[way * HALF : (way + 1) * HALF]

    def near_send(name, way, out, arrive, at):
        rows = [chunk(1 - way, k) for k in range(CHUNKS)]
        return [
            remote((name, "n", way, k), out.at[rows[k], :], arrive.at[way, rows[k], :], at(1 if way == 0 else -1))
            for k in range(CHUNKS)
        ]

    def relay_send(name, far_in, way, k, out, keep, relay, arrive, at):
        far_in[way][k].wait_recv()
        inner = pl.ds(k * CHUNK, CHUNK)
        outer = chunk(way, k)
        out[outer, :] = (keep[way, inner, :] + relay[way, inner, :].astype(F32)).astype(BF16)
        return remote((name, "s", way, k), out.at[outer, :], arrive.at[way, outer, :], at(1 if way == 0 else -1))

    def finish(near, sums, way, k, own, arrive, out, result, sem):
        near[1 - way][k].wait_recv()
        sums[way][k].wait_recv()
        rows = chunk(way, k)
        out[rows, :] = (
            own[rows, :] + arrive[0, rows, :].astype(F32) + arrive[1, rows, :].astype(F32)
        ).astype(BF16)
        copy = pltpu.make_async_copy(out.at[rows, :], result.at[rows, :], local_sem.at[sem])
        copy.start()
        return copy

    x2_feats = ds(ring(x, 2) * FEATS, FEATS, FEATS)

    def back_of(q):
        cols = ds(q * COLS, COLS, 128)
        return lax.dot_general(cot_g[:, cols], uu[:, cols], TRANSPOSED, preferred_element_type=F32)

    def x2_of(q):
        cols = ds(q * COLS, COLS, 128)
        return lax.dot_general(cot_g[:, cols], wg[x2_feats, cols], TRANSPOSED, preferred_element_type=F32)

    core_wait(2)
    loads[5].wait()
    y_far_in = far_send("y", project(ring(y, 2)), y_far, y_relay, at_y)
    z_relay(3, z3)
    y_own[...] = project(y)
    z_near(3, z3)
    z_relay(1, z1)
    loads[4].wait()
    x2_part[...] = x2_of(y)
    z_far(3, z3)
    z_near(1, z1)
    z_far(1, z1)
    core_wait(3)
    arrived(("cot", "second"))
    back_part[...] = back_of(y) + back_of(ring(y, 1)) + back_of(ring(y, -1))
    x2_part[...] += x2_of(ring(y, 1))
    core_wait(1)
    x2_part[...] += x2_of(ring(y, -1))
    near_compute(project(ring(y, 1)), 0, y_plus, y_keep)

    arrived(("cot", "relay"))
    split_gated(back_part[...] + back_of(ring(y, 2)), back_hl)
    x2_value = x2_part[...] + x2_of(ring(y, 2)) + jnp.dot(
        back_hl[...], dd[:, ds(ring(x, 2) * FEATS, FEATS, 128)], preferred_element_type=F32
    )
    x_far_in = far_send("x", x2_value, x_far, x_relay, at_x)
    y_near = [near_send("y", 0, y_plus, y_in, at_y)]
    near_compute(project(ring(y, -1)), 1, y_minus, y_keep)
    y_near.append(near_send("y", 1, y_minus, y_in, at_y))
    near_compute(input_grad(ring(x, 1)), 0, x_plus, x_keep)
    x_near = [near_send("x", 0, x_plus, x_in, at_x)]
    near_compute(input_grad(ring(x, -1)), 1, x_minus, x_keep)
    x_near.append(near_send("x", 1, x_minus, x_in, at_x))
    x_own[...] = input_grad(x)
    y_sums, x_sums = ([], []), ([], [])
    for k in range(CHUNKS):
        y_sums[0].append(relay_send("y", y_far_in, 0, k, y_plus, y_keep, y_relay, y_in, at_y))
        y_sums[1].append(relay_send("y", y_far_in, 1, k, y_minus, y_keep, y_relay, y_in, at_y))
        x_sums[0].append(relay_send("x", x_far_in, 0, k, x_plus, x_keep, x_relay, x_in, at_x))
        x_sums[1].append(relay_send("x", x_far_in, 1, k, x_minus, x_keep, x_relay, x_in, at_x))
    last = []
    for k in range(CHUNKS):
        for way in (0, 1):
            last.append(finish(x_near, x_sums, way, k, x_own, x_in, x_out, grad_tokens, len(loads) + len(last)))
        for way in (0, 1):
            last.append(finish(y_near, y_sums, way, k, y_own, y_in, y_out, projected, len(loads) + len(last)))
    for copy in last:
        copy.wait()
    for kind, size in sent.items():
        wait_for(kind, size, send_sem.at[send_index[kind]])
    assert len(send_index) == N_SEND and len(recv_index) == N_RECV


def copy_kernel(a, b, a_out, b_out, a_v, b_v, in_sems, out_sems):
    pairs = []
    for i, (src, held, dst) in enumerate(((a, a_v, a_out), (b, b_v, b_out))):
        for k in range(COPIES):
            rows = pl.ds(k * (GROUP // COPIES), GROUP // COPIES)
            pairs.append((
                pltpu.make_async_copy(src.at[rows, :], held.at[rows, :], in_sems.at[i, k]),
                pltpu.make_async_copy(held.at[rows, :], dst.at[rows, :], out_sems.at[i, k]),
            ))
    for fetch, _ in pairs:
        fetch.start()
    for fetch, store in pairs:
        fetch.wait()
        store.start()
    for _, store in pairs:
        store.wait()


def per_device(tokens, cotangent, gates, weight, down, up, expert, store_row):
    any_space = pl.BlockSpec(memory_space=pl.ANY)

    def ring_scratch(width):
        return [
            pltpu.VMEM((GROUP, width), BF16),
            pltpu.VMEM((GROUP, width), BF16),
            pltpu.VMEM((GROUP, width), BF16),
            pltpu.VMEM((2, HALF, width), F32),
            pltpu.VMEM((GROUP, width), F32),
            pltpu.VMEM((2, HALF, width), BF16),
            pltpu.VMEM((2, GROUP, width), BF16),
            pltpu.VMEM((GROUP, width), BF16),
        ]

    flops = 2 * 2 * GROUP * ROW_FEATS * ROW_COLS
    outs = (
        jax.ShapeDtypeStruct((GROUP, COLS), BF16),
        jax.ShapeDtypeStruct((GROUP, FEATS), BF16),
    )
    result = pl.pallas_call(
        kernel,
        out_shape=outs,
        in_specs=[any_space] * 8,
        out_specs=(any_space, any_space),
        scratch_shapes=[
            pltpu.VMEM((ROW_FEATS, ROW_COLS), BF16),
            pltpu.VMEM((GROUP, ROW_FEATS), BF16),
            pltpu.VMEM((GROUP, ROW_COLS), BF16),
            pltpu.VMEM((USED, GROUP), F32),
            pltpu.VMEM((2 * LOW, GROUP), F32),
            pltpu.VMEM((GROUP, 2 * LOW), F32),
            pltpu.VMEM((STORED, RANK, FEATS), BF16),
            pltpu.VMEM((STORED, RANK, COLS), BF16),
            pltpu.VMEM((SEQ * CAP, RANK, FEATS + COLS), BF16),
            pltpu.VMEM((SEQ * CAP, RANK, FEATS + COLS), BF16),
            pltpu.VMEM((2 * LOW, ROW_FEATS), BF16),
            pltpu.VMEM((2 * LOW, ROW_COLS), BF16),
            pltpu.VMEM((GROUP, 2 * LOW), BF16),
            pltpu.VMEM((GROUP, 2 * LOW), BF16),
            pltpu.VMEM((GROUP, 2 * LOW), F32),
            pltpu.VMEM((GROUP, FEATS), F32),
        ]
        + ring_scratch(COLS)
        + ring_scratch(FEATS)
        + [
            pltpu.SMEM((USED, SEQ), jnp.int32),
            pltpu.SMEM((SEQ * STORED,), jnp.int32),
            pltpu.SemaphoreType.DMA((8 + 4 * CHUNKS,)),
            pltpu.SemaphoreType.DMA((N_SEND,)),
            pltpu.SemaphoreType.DMA((N_RECV,)),
        ],
        compiler_params=pltpu.CompilerParams(
            collective_id=0, has_side_effects=True, vmem_limit_bytes=60 * 2**20
        ),
        cost_estimate=pl.CostEstimate(flops=flops, bytes_accessed=20 * 2**20, transcendentals=0),
        name="mixture",
    )(tokens, cotangent, gates.T, weight, down, up, expert.T, store_row)
    return pl.pallas_call(
        copy_kernel,
        out_shape=outs,
        in_specs=[any_space] * 2,
        out_specs=(any_space, any_space),
        scratch_shapes=[
            pltpu.VMEM((GROUP, COLS), BF16),
            pltpu.VMEM((GROUP, FEATS), BF16),
            pltpu.SemaphoreType.DMA((2, COPIES)),
            pltpu.SemaphoreType.DMA((2, COPIES)),
        ],
        compiler_params=pltpu.CompilerParams(vmem_limit_bytes=60 * 2**20),
        name="results",
    )(*result)


def solution(mesh):
    return jax.shard_map(
        per_device,
        mesh=mesh,
        in_specs=(
            P("seq", "tensor"),
            P("seq", "tensor"),
            P("seq", None),
            P(None, "tensor"),
            P("seq", None, "tensor"),
            P("seq", None, "tensor"),
            P(),
            P(),
        ),
        out_specs=(P("seq", "tensor"), P("seq", "tensor")),
        check_vma=False,
    )
```

```python
import math

import jax
import jax.numpy as jnp
from jax import lax
from jax.experimental import pallas as pl
from jax.experimental.pallas import tpu as pltpu
from jax.sharding import PartitionSpec as P

F32 = jnp.float32
BF16 = jnp.bfloat16
MESH = pl.DeviceIdType.MESH
RING = 4
CORES = 2
GROUP = 768
HALF = GROUP // 2
FEATS = 512
COLS = 640
ROW_FEATS = RING * FEATS
ROW_COLS = RING * COLS
RANK = 16
USED = 4
LOW = USED * RANK
STORED = 128
SEQ = RING * CORES
CAP = 2
PIECE = FEATS // CORES
PART = PIECE // 2
CHUNKS = 3
CHUNK = HALF // CHUNKS
TRANSPOSED = (((1,), (1,)), ((), ()))
N_SEND = 10
N_RECV = 67
COPIES = 2


def ds(start, size, align):
    return pl.ds(pl.multiple_of(start, align), size)


def kernel(
    tok, cot, gates, weight, down, up, expert_in, store_row_in,
    projected, grad_tokens,
    wg, tok_g, cot_g, gate_v, gate_t, gate, down_v, up_v, ad_send, ad_recv, dd, uu, low_hl, back_hl,
    back_part, x2_part,
    y_far, y_plus, y_minus, y_keep, y_own, y_relay, y_in, y_out,
    x_far, x_plus, x_minus, x_keep, x_own, x_relay, x_in, x_out,
    expert, store_row, local_sem, send_sem, recv_sem,
):
    seq, ten = lax.axis_index("seq"), lax.axis_index("tensor")
    z, c = seq // CORES, lax.rem(seq, CORES)
    y, x = ten // RING, lax.rem(ten, RING)

    def ring(value, step):
        return lax.rem(value + (step + RING), RING)

    def at_x(step):
        return (seq, y * RING + ring(x, step))

    def at_y(step):
        return (seq, ring(y, step) * RING + x)

    def at_z(step):
        return (ring(z, step) * CORES + c, ten)

    other_core = (z * CORES + (1 - c), ten)

    def at_seq(step):
        return (lax.rem(seq + step, SEQ), ten)

    barrier = pltpu.get_barrier_semaphore()
    partners = [at_x(s) for s in (1, 2, 3)] + [at_y(s) for s in (1, 2, 3)]
    partners += [at_seq(s) for s in range(1, SEQ)]
    for partner in partners:
        pl.semaphore_signal(barrier, inc=1, device_id=partner, device_id_type=MESH)

    rows_y = ds(y * ROW_FEATS, ROW_FEATS, ROW_FEATS)
    cols_x = ds(x * FEATS, FEATS, 128)
    cols_y = ds(y * COLS, COLS, 128)
    loads = [
        (down, down_v), (up, up_v), (gates, gate_v),
        (tok, tok_g.at[:, cols_x]), (cot, cot_g.at[:, cols_y]),
        (weight.at[rows_y, :], wg.at[:, cols_y]), (expert_in, expert), (store_row_in, store_row),
    ]
    loads = [pltpu.make_async_copy(s, d, local_sem.at[i]) for i, (s, d) in enumerate(loads)]
    for load in loads[6:] + loads[:2]:
        load.start()

    send_index, recv_index, sent, received = {}, {}, {}, {}

    def remote(name, src, dst, device, together=None):
        kind, key = name[0], name if together is None else together
        copy = pltpu.make_async_remote_copy(
            src_ref=src,
            dst_ref=dst,
            send_sem=send_sem.at[send_index.setdefault(kind, len(send_index))],
            recv_sem=recv_sem.at[recv_index.setdefault(key, len(recv_index))],
            device_id=device,
            device_id_type=MESH,
        )
        copy.start()
        size = math.prod(src.shape)
        sent[kind] = sent.get(kind, 0) + size
        received[key] = received.get(key, 0) + size
        return copy

    def wait_for(kind, size, sem):
        if kind == "ad":
            whole = ad_send.at[pl.ds(0, size // math.prod(ad_send.shape[1:]))]
        else:
            array = tok_g if kind in ("tok", "x", "down") else wg
            whole = array.at[pl.ds(0, size // array.shape[1]), :]
        pltpu.make_async_copy(whole, whole, sem).wait()

    def arrived(key):
        wait_for(key[0], received[key], recv_sem.at[recv_index[key]])

    pl.semaphore_wait(barrier, len(partners))

    my_rows = ds(z * FEATS + c * PIECE, PIECE, PIECE)
    w_in = {}
    for step in (2, 1, 3):
        first = ring(y, step) * ROW_FEATS + z * FEATS + c * PIECE
        w_in[step] = remote(
            ("w", step), weight.at[ds(first, PIECE, PIECE), :], wg.at[my_rows, cols_y], at_y(step)
        )

    def chunk(half, k):
        return pl.ds(half * HALF + k * CHUNK, CHUNK)

    def gather_own(name, way, half, src, dst, cols, at, together=None):
        return [
            remote((name, way, half, k), src.at[chunk(half, k), :], dst.at[chunk(half, k), cols], at(1 if way == 0 else -1), together)
            for k in range(CHUNKS)
        ]

    def gather_first(name, src, dst, cols, at):
        return [gather_own(name, way, way, src, dst, cols, at) for way in (0, 1)]

    def gather_second(name, src, dst, cols, at):
        for way in (0, 1):
            gather_own(name, way, 1 - way, src, dst, cols, at, (name, "second"))

    def gather_relay(name, first, dst, pos, width, at):
        for k in range(CHUNKS):
            for way in (0, 1):
                first[way][k].wait_recv()
                step = 1 if way == 0 else -1
                here = dst.at[chunk(way, k), ds(ring(pos, -step) * width, width, 128)]
                remote((name, "r", way, k), here, here, at(step), (name, "relay"))

    tok_first = gather_first("tok", tok, tok_g, cols_x, at_x)
    gather_second("tok", tok, tok_g, cols_x, at_x)

    for load in loads[2:6]:
        load.start()

    for load in loads[6:] + loads[:2]:
        load.wait()

    def fill(g, carry):
        picks = [jnp.int32(0)] * CAP
        count = jnp.int32(0)
        for j in range(USED):
            local = store_row[expert[j, g]] - seq * STORED
            mine = (local >= 0) & (local < STORED)
            for k in range(CAP):
                picks[k] = jnp.where(mine & (count == k), local, picks[k])
            count = count + mine.astype(jnp.int32)
        for k in range(CAP):
            ad_send[g * CAP + k, :, :FEATS] = down_v[picks[k]]
            ad_send[g * CAP + k, :, FEATS:] = up_v[picks[k]]
        return carry

    lax.fori_loop(0, SEQ, fill, 0)
    mine_slots = pl.ds(seq * CAP, CAP)
    for step in range(1, SEQ):
        target = at_seq(step)
        remote(("ad",), ad_send.at[pl.ds(target[0] * CAP, CAP)], ad_recv.at[mine_slots], target)
    for k in range(CAP):
        ad_recv[seq * CAP + k] = ad_send[seq * CAP + k]

    def to_core(step, place):
        remote(("core", step), place, place, other_core)

    def z_place(zz, q, part=None):
        first = zz * FEATS + c * PIECE + (0 if part is None else part * PART)
        return wg.at[ds(first, PIECE if part is None else PART, PART), ds(q * COLS, COLS, 128)]

    def z_start(step):
        w_in[step].wait_recv()
        q = ring(y, -step)
        n = lambda k: ("z", step, k)
        out = {}
        for part in (0, 1):
            here = z_place(z, q, part)
            together = None if part == 0 else ("z", step, "near")
            out["p", part] = remote(n(("p", part)), here, here, at_z(1), together)
            here = z_place(z, q, 1 - part)
            out["m", 1 - part] = remote(n(("m", 1 - part)), here, here, at_z(-1), together)
        to_core(step, z_place(z, q))
        return out

    def z_relay(step, out):
        q = ring(y, -step)
        out["p", 0].wait_recv()
        here = z_place(ring(z, -1), q, 0)
        remote(("z", step, "far"), here, here, at_z(1))
        out["m", 1].wait_recv()
        here = z_place(ring(z, 1), q, 1)
        remote(("z", step, "far"), here, here, at_z(-1))

    def z_near(step):
        q = ring(y, -step)
        arrived(("z", step, "near"))
        to_core(step, z_place(ring(z, -1), q))
        to_core(step, z_place(ring(z, 1), q))

    def z_far(step):
        q = ring(y, -step)
        arrived(("z", step, "far"))
        to_core(step, z_place(ring(z, 2), q))

    def core_wait(step):
        arrived(("core", step))

    z2 = z_start(2)
    gather_relay("tok", tok_first, tok_g, x, FEATS, at_x)

    arrived(("ad",))
    holders = []
    for j in range(USED):
        holder = store_row[expert[j, seq]] // STORED
        rank = jnp.int32(0)
        for earlier in holders:
            rank = rank + (earlier == holder).astype(jnp.int32)
        holders.append(holder)
        rows = ad_recv[holder * CAP + rank]
        dd[pl.ds(j * RANK, RANK), cols_x] = rows[:, :FEATS]
        uu[pl.ds(j * RANK, RANK), cols_y] = rows[:, FEATS:]
    low_rows = pl.ds(0, LOW)
    low_half = (pl.ds(0, LOW // 2), pl.ds(LOW // 2, LOW // 2))
    up_first = []
    for way in (0, 1):
        here = uu.at[low_half[way], cols_y]
        up_first.append(remote(("up", way), here, here, at_y(1 - 2 * way)))
    for way in (0, 1):
        here = uu.at[low_half[1 - way], cols_y]
        remote(("up", "rest"), here, here, at_y(1 - 2 * way))
    cot_first = gather_first("cot", cot, cot_g, cols_y, at_y)
    for step in (2, 1, 3):
        here = dd.at[low_rows, cols_x]
        remote(("down",), here, here, at_x(step))

    z_relay(2, z2)
    z3 = z_start(3)
    z1 = z_start(1)
    for way in (0, 1):
        up_first[way].wait_recv()
        here = uu.at[low_half[way], ds(ring(y, 2 * way - 1) * COLS, COLS, 128)]
        remote(("up", "rest"), here, here, at_y(1 - 2 * way))
    gather_second("cot", cot, cot_g, cols_y, at_y)
    z_near(2)
    z_far(2)

    loads[2].wait()
    for j in range(USED):
        row = jnp.broadcast_to(gate_v[pl.ds(j, 1), :], (RANK, GROUP))
        gate_t[pl.ds(j * RANK, RANK), :] = row
        gate_t[pl.ds(LOW + j * RANK, RANK), :] = row
    gate[...] = gate_t[...].T
    first_half = lax.broadcasted_iota(jnp.int32, (GROUP, 2 * LOW), 1) < LOW

    def split_gated(value, out):
        gated = value * gate[...]
        high = gated.astype(BF16).astype(F32)
        out[...] = jnp.where(first_half, high, gated - high).astype(BF16)

    arrived(("tok", "second"))
    arrived(("tok", "relay"))
    loads[3].wait()
    gather_relay("cot", cot_first, cot_g, y, COLS, at_y)
    arrived(("down",))
    arrived(("up", "rest"))
    dd[LOW:, :] = dd[:LOW, :]
    uu[LOW:, :] = uu[:LOW, :]
    split_gated(
        lax.dot_general(tok_g[...], dd[...], TRANSPOSED, preferred_element_type=F32), low_hl
    )

    def project(q):
        cols = ds(q * COLS, COLS, 128)
        return jnp.dot(tok_g[...], wg[:, cols], preferred_element_type=F32) + jnp.dot(
            low_hl[...], uu[:, cols], preferred_element_type=F32
        )

    def input_grad(q):
        feats = ds(q * FEATS, FEATS, FEATS)
        return lax.dot_general(
            cot_g[...], wg[feats, :], TRANSPOSED, preferred_element_type=F32
        ) + jnp.dot(
            back_hl[...], dd[:, ds(q * FEATS, FEATS, 128)], preferred_element_type=F32
        )

    def far_send(name, value, far, relay, at):
        far[...] = value.astype(BF16)
        return [
            [
                remote((name, "f", way, k), far.at[chunk(way, k), :], relay.at[way, pl.ds(k * CHUNK, CHUNK), :], at(1 if way == 0 else -1))
                for k in range(CHUNKS)
            ]
            for way in (0, 1)
        ]

    def near_compute(value, way, out, keep):
        direct = 1 - way
        out[pl.ds(direct * HALF, HALF), :] = value[direct * HALF : (direct + 1) * HALF].astype(BF16)
        keep[way] = value[way * HALF : (way + 1) * HALF]

    def near_send(name, way, out, arrive, at):
        rows = [chunk(1 - way, k) for k in range(CHUNKS)]
        for row in rows:
            remote((name, "n", way), out.at[row, :], arrive.at[way, row, :], at(1 if way == 0 else -1))

    def relay_send(name, far_in, way, k, out, keep, relay, arrive, at):
        far_in[way][k].wait_recv()
        inner = pl.ds(k * CHUNK, CHUNK)
        outer = chunk(way, k)
        out[outer, :] = (keep[way, inner, :] + relay[way, inner, :].astype(F32)).astype(BF16)
        return remote((name, "s", way, k), out.at[outer, :], arrive.at[way, outer, :], at(1 if way == 0 else -1))

    def finish(sums, way, k, own, arrive, out, result, sem):
        sums[way][k].wait_recv()
        rows = chunk(way, k)
        out[rows, :] = (
            own[rows, :] + arrive[0, rows, :].astype(F32) + arrive[1, rows, :].astype(F32)
        ).astype(BF16)
        copy = pltpu.make_async_copy(out.at[rows, :], result.at[rows, :], local_sem.at[sem])
        copy.start()
        return copy

    x2_feats = ds(ring(x, 2) * FEATS, FEATS, FEATS)

    def back_of(q):
        cols = ds(q * COLS, COLS, 128)
        return lax.dot_general(cot_g[:, cols], uu[:, cols], TRANSPOSED, preferred_element_type=F32)

    def x2_of(q):
        cols = ds(q * COLS, COLS, 128)
        return lax.dot_general(cot_g[:, cols], wg[x2_feats, cols], TRANSPOSED, preferred_element_type=F32)

    core_wait(2)
    loads[5].wait()
    y_far_in = far_send("y", project(ring(y, 2)), y_far, y_relay, at_y)
    z_relay(3, z3)
    y_own[...] = project(y)
    z_near(3)
    z_relay(1, z1)
    loads[4].wait()
    x2_part[...] = x2_of(y)
    z_far(3)
    z_near(1)
    z_far(1)
    core_wait(3)
    arrived(("cot", "second"))
    back_part[...] = back_of(y) + back_of(ring(y, 1)) + back_of(ring(y, -1))
    x2_part[...] += x2_of(ring(y, 1))
    core_wait(1)
    x2_part[...] += x2_of(ring(y, -1))
    near_compute(project(ring(y, 1)), 0, y_plus, y_keep)

    arrived(("cot", "relay"))
    split_gated(back_part[...] + back_of(ring(y, 2)), back_hl)
    x2_value = x2_part[...] + x2_of(ring(y, 2)) + jnp.dot(
        back_hl[...], dd[:, ds(ring(x, 2) * FEATS, FEATS, 128)], preferred_element_type=F32
    )
    x_far_in = far_send("x", x2_value, x_far, x_relay, at_x)
    near_send("y", 0, y_plus, y_in, at_y)
    near_compute(project(ring(y, -1)), 1, y_minus, y_keep)
    near_send("y", 1, y_minus, y_in, at_y)
    near_compute(input_grad(ring(x, 1)), 0, x_plus, x_keep)
    near_send("x", 0, x_plus, x_in, at_x)
    near_compute(input_grad(ring(x, -1)), 1, x_minus, x_keep)
    near_send("x", 1, x_minus, x_in, at_x)
    x_own[...] = input_grad(x)
    y_sums, x_sums = ([], []), ([], [])
    for k in range(CHUNKS):
        y_sums[0].append(relay_send("y", y_far_in, 0, k, y_plus, y_keep, y_relay, y_in, at_y))
        y_sums[1].append(relay_send("y", y_far_in, 1, k, y_minus, y_keep, y_relay, y_in, at_y))
        x_sums[0].append(relay_send("x", x_far_in, 0, k, x_plus, x_keep, x_relay, x_in, at_x))
        x_sums[1].append(relay_send("x", x_far_in, 1, k, x_minus, x_keep, x_relay, x_in, at_x))
    for name in ("x", "y"):
        for way in (0, 1):
            arrived((name, "n", way))
    last = []
    for k in range(CHUNKS):
        for way in (0, 1):
            last.append(finish(x_sums, way, k, x_own, x_in, x_out, grad_tokens, len(loads) + len(last)))
        for way in (0, 1):
            last.append(finish(y_sums, way, k, y_own, y_in, y_out, projected, len(loads) + len(last)))
    for copy in last:
        copy.wait()
    for kind, size in sent.items():
        wait_for(kind, size, send_sem.at[send_index[kind]])
    assert len(send_index) == N_SEND and len(recv_index) == N_RECV


def copy_kernel(a, b, a_out, b_out, a_v, b_v, in_sems, out_sems):
    pairs = []
    for i, (src, held, dst) in enumerate(((a, a_v, a_out), (b, b_v, b_out))):
        for k in range(COPIES):
            rows = pl.ds(k * (GROUP // COPIES), GROUP // COPIES)
            pairs.append((
                pltpu.make_async_copy(src.at[rows, :], held.at[rows, :], in_sems.at[i, k]),
                pltpu.make_async_copy(held.at[rows, :], dst.at[rows, :], out_sems.at[i, k]),
            ))
    for fetch, _ in pairs:
        fetch.start()
    for fetch, store in pairs:
        fetch.wait()
        store.start()
    for _, store in pairs:
        store.wait()


def per_device(tokens, cotangent, gates, weight, down, up, expert, store_row):
    any_space = pl.BlockSpec(memory_space=pl.ANY)

    def ring_scratch(width):
        return [
            pltpu.VMEM((GROUP, width), BF16),
            pltpu.VMEM((GROUP, width), BF16),
            pltpu.VMEM((GROUP, width), BF16),
            pltpu.VMEM((2, HALF, width), F32),
            pltpu.VMEM((GROUP, width), F32),
            pltpu.VMEM((2, HALF, width), BF16),
            pltpu.VMEM((2, GROUP, width), BF16),
            pltpu.VMEM((GROUP, width), BF16),
        ]

    flops = 2 * 2 * GROUP * ROW_FEATS * ROW_COLS
    outs = (
        jax.ShapeDtypeStruct((GROUP, COLS), BF16),
        jax.ShapeDtypeStruct((GROUP, FEATS), BF16),
    )
    result = pl.pallas_call(
        kernel,
        out_shape=outs,
        in_specs=[any_space] * 8,
        out_specs=(any_space, any_space),
        scratch_shapes=[
            pltpu.VMEM((ROW_FEATS, ROW_COLS), BF16),
            pltpu.VMEM((GROUP, ROW_FEATS), BF16),
            pltpu.VMEM((GROUP, ROW_COLS), BF16),
            pltpu.VMEM((USED, GROUP), F32),
            pltpu.VMEM((2 * LOW, GROUP), F32),
            pltpu.VMEM((GROUP, 2 * LOW), F32),
            pltpu.VMEM((STORED, RANK, FEATS), BF16),
            pltpu.VMEM((STORED, RANK, COLS), BF16),
            pltpu.VMEM((SEQ * CAP, RANK, FEATS + COLS), BF16),
            pltpu.VMEM((SEQ * CAP, RANK, FEATS + COLS), BF16),
            pltpu.VMEM((2 * LOW, ROW_FEATS), BF16),
            pltpu.VMEM((2 * LOW, ROW_COLS), BF16),
            pltpu.VMEM((GROUP, 2 * LOW), BF16),
            pltpu.VMEM((GROUP, 2 * LOW), BF16),
            pltpu.VMEM((GROUP, 2 * LOW), F32),
            pltpu.VMEM((GROUP, FEATS), F32),
        ]
        + ring_scratch(COLS)
        + ring_scratch(FEATS)
        + [
            pltpu.SMEM((USED, SEQ), jnp.int32),
            pltpu.SMEM((SEQ * STORED,), jnp.int32),
            pltpu.SemaphoreType.DMA((8 + 4 * CHUNKS,)),
            pltpu.SemaphoreType.DMA((N_SEND,)),
            pltpu.SemaphoreType.DMA((N_RECV,)),
        ],
        compiler_params=pltpu.CompilerParams(
            collective_id=0, has_side_effects=True, vmem_limit_bytes=60 * 2**20
        ),
        cost_estimate=pl.CostEstimate(flops=flops, bytes_accessed=20 * 2**20, transcendentals=0),
        name="mixture",
    )(tokens, cotangent, gates.T, weight, down, up, expert.T, store_row)
    return pl.pallas_call(
        copy_kernel,
        out_shape=outs,
        in_specs=[any_space] * 2,
        out_specs=(any_space, any_space),
        scratch_shapes=[
            pltpu.VMEM((GROUP, COLS), BF16),
            pltpu.VMEM((GROUP, FEATS), BF16),
            pltpu.SemaphoreType.DMA((2, COPIES)),
            pltpu.SemaphoreType.DMA((2, COPIES)),
        ],
        compiler_params=pltpu.CompilerParams(vmem_limit_bytes=60 * 2**20),
        name="results",
    )(*result)


def solution(mesh):
    return jax.shard_map(
        per_device,
        mesh=mesh,
        in_specs=(
            P("seq", "tensor"),
            P("seq", "tensor"),
            P("seq", None),
            P(None, "tensor"),
            P("seq", None, "tensor"),
            P("seq", None, "tensor"),
            P(),
            P(),
        ),
        out_specs=(P("seq", "tensor"), P("seq", "tensor")),
        check_vma=False,
    )
```

```python
import math

import jax
import jax.numpy as jnp
from jax import lax
from jax.experimental import pallas as pl
from jax.experimental.pallas import tpu as pltpu
from jax.sharding import PartitionSpec as P

F32 = jnp.float32
BF16 = jnp.bfloat16
MESH = pl.DeviceIdType.MESH
RING = 4
CORES = 2
GROUP = 768
HALF = GROUP // 2
FEATS = 512
COLS = 640
ROW_FEATS = RING * FEATS
ROW_COLS = RING * COLS
RANK = 16
USED = 4
LOW = USED * RANK
STORED = 128
SEQ = RING * CORES
CAP = 2
PIECE = FEATS // CORES
PART = PIECE // 2
CHUNKS = 3
CHUNK = HALF // CHUNKS
SUMS = ((0, CHUNK), (CHUNK, CHUNK), (2 * CHUNK, CHUNK * 3 // 4), (2 * CHUNK + CHUNK * 3 // 4, CHUNK // 4))
TRANSPOSED = (((1,), (1,)), ((), ()))
N_SEND = 10
N_RECV = 71
COPIES = 2


def ds(start, size, align):
    return pl.ds(pl.multiple_of(start, align), size)


def kernel(
    tok, cot, gates, weight, down, up, expert_in, store_row_in,
    projected, grad_tokens,
    wg, tok_g, cot_g, gate_v, gate_t, gate, down_v, up_v, ad_send, ad_recv, dd, uu, low_hl, back_hl,
    back_part, x2_part,
    y_far, y_plus, y_minus, y_keep, y_own, y_relay, y_in, y_out,
    x_far, x_plus, x_minus, x_keep, x_own, x_relay, x_in, x_out,
    expert, store_row, local_sem, send_sem, recv_sem,
):
    seq, ten = lax.axis_index("seq"), lax.axis_index("tensor")
    z, c = seq // CORES, lax.rem(seq, CORES)
    y, x = ten // RING, lax.rem(ten, RING)

    def ring(value, step):
        return lax.rem(value + (step + RING), RING)

    def at_x(step):
        return (seq, y * RING + ring(x, step))

    def at_y(step):
        return (seq, ring(y, step) * RING + x)

    def at_z(step):
        return (ring(z, step) * CORES + c, ten)

    other_core = (z * CORES + (1 - c), ten)

    def at_seq(step):
        return (lax.rem(seq + step, SEQ), ten)

    barrier = pltpu.get_barrier_semaphore()
    partners = [at_x(s) for s in (1, 2, 3)] + [at_y(s) for s in (1, 2, 3)]
    partners += [at_seq(s) for s in range(1, SEQ)]
    for partner in partners:
        pl.semaphore_signal(barrier, inc=1, device_id=partner, device_id_type=MESH)

    rows_y = ds(y * ROW_FEATS, ROW_FEATS, ROW_FEATS)
    cols_x = ds(x * FEATS, FEATS, 128)
    cols_y = ds(y * COLS, COLS, 128)
    loads = [
        (down, down_v), (up, up_v), (gates, gate_v),
        (tok, tok_g.at[:, cols_x]), (cot, cot_g.at[:, cols_y]),
        (weight.at[rows_y, :], wg.at[:, cols_y]), (expert_in, expert), (store_row_in, store_row),
    ]
    loads = [pltpu.make_async_copy(s, d, local_sem.at[i]) for i, (s, d) in enumerate(loads)]
    for load in loads[6:] + loads[:2]:
        load.start()

    send_index, recv_index, sent, received = {}, {}, {}, {}

    def remote(name, src, dst, device, together=None):
        kind, key = name[0], name if together is None else together
        copy = pltpu.make_async_remote_copy(
            src_ref=src,
            dst_ref=dst,
            send_sem=send_sem.at[send_index.setdefault(kind, len(send_index))],
            recv_sem=recv_sem.at[recv_index.setdefault(key, len(recv_index))],
            device_id=device,
            device_id_type=MESH,
        )
        copy.start()
        size = math.prod(src.shape)
        sent[kind] = sent.get(kind, 0) + size
        received[key] = received.get(key, 0) + size
        return copy

    def wait_for(kind, size, sem):
        if kind == "ad":
            whole = ad_send.at[pl.ds(0, size // math.prod(ad_send.shape[1:]))]
        else:
            array = tok_g if kind in ("tok", "x", "down") else wg
            whole = array.at[pl.ds(0, size // array.shape[1]), :]
        pltpu.make_async_copy(whole, whole, sem).wait()

    def arrived(key):
        wait_for(key[0], received[key], recv_sem.at[recv_index[key]])

    pl.semaphore_wait(barrier, len(partners))

    my_rows = ds(z * FEATS + c * PIECE, PIECE, PIECE)
    w_in = {}
    for step in (2, 1, 3):
        first = ring(y, step) * ROW_FEATS + z * FEATS + c * PIECE
        w_in[step] = remote(
            ("w", step), weight.at[ds(first, PIECE, PIECE), :], wg.at[my_rows, cols_y], at_y(step)
        )

    def chunk(half, k):
        return pl.ds(half * HALF + k * CHUNK, CHUNK)

    def gather_own(name, way, half, src, dst, cols, at, together=None):
        return [
            remote((name, way, half, k), src.at[chunk(half, k), :], dst.at[chunk(half, k), cols], at(1 if way == 0 else -1), together)
            for k in range(CHUNKS)
        ]

    def gather_first(name, src, dst, cols, at):
        return [gather_own(name, way, way, src, dst, cols, at) for way in (0, 1)]

    def gather_second(name, src, dst, cols, at):
        for way in (0, 1):
            gather_own(name, way, 1 - way, src, dst, cols, at, (name, "second"))

    def gather_relay(name, first, dst, pos, width, at):
        for k in range(CHUNKS):
            for way in (0, 1):
                first[way][k].wait_recv()
                step = 1 if way == 0 else -1
                here = dst.at[chunk(way, k), ds(ring(pos, -step) * width, width, 128)]
                remote((name, "r", way, k), here, here, at(step), (name, "relay"))

    tok_first = gather_first("tok", tok, tok_g, cols_x, at_x)
    gather_second("tok", tok, tok_g, cols_x, at_x)

    for load in loads[2:6]:
        load.start()

    for load in loads[6:] + loads[:2]:
        load.wait()

    def fill(g, carry):
        picks = [jnp.int32(0)] * CAP
        count = jnp.int32(0)
        for j in range(USED):
            local = store_row[expert[j, g]] - seq * STORED
            mine = (local >= 0) & (local < STORED)
            for k in range(CAP):
                picks[k] = jnp.where(mine & (count == k), local, picks[k])
            count = count + mine.astype(jnp.int32)
        for k in range(CAP):
            ad_send[g * CAP + k, :, :FEATS] = down_v[picks[k]]
            ad_send[g * CAP + k, :, FEATS:] = up_v[picks[k]]
        return carry

    lax.fori_loop(0, SEQ, fill, 0)
    mine_slots = pl.ds(seq * CAP, CAP)
    for step in range(1, SEQ):
        target = at_seq(step)
        remote(("ad",), ad_send.at[pl.ds(target[0] * CAP, CAP)], ad_recv.at[mine_slots], target)
    for k in range(CAP):
        ad_recv[seq * CAP + k] = ad_send[seq * CAP + k]

    def to_core(step, place):
        remote(("core", step), place, place, other_core)

    def z_place(zz, q, part=None):
        first = zz * FEATS + c * PIECE + (0 if part is None else part * PART)
        return wg.at[ds(first, PIECE if part is None else PART, PART), ds(q * COLS, COLS, 128)]

    def z_start(step):
        w_in[step].wait_recv()
        q = ring(y, -step)
        n = lambda k: ("z", step, k)
        out = {}
        for part in (0, 1):
            here = z_place(z, q, part)
            together = None if part == 0 else ("z", step, "near")
            out["p", part] = remote(n(("p", part)), here, here, at_z(1), together)
            here = z_place(z, q, 1 - part)
            out["m", 1 - part] = remote(n(("m", 1 - part)), here, here, at_z(-1), together)
        to_core(step, z_place(z, q))
        return out

    def z_relay(step, out):
        q = ring(y, -step)
        out["p", 0].wait_recv()
        here = z_place(ring(z, -1), q, 0)
        remote(("z", step, "far"), here, here, at_z(1))
        out["m", 1].wait_recv()
        here = z_place(ring(z, 1), q, 1)
        remote(("z", step, "far"), here, here, at_z(-1))

    def z_near(step):
        q = ring(y, -step)
        arrived(("z", step, "near"))
        to_core(step, z_place(ring(z, -1), q))
        to_core(step, z_place(ring(z, 1), q))

    def z_far(step):
        q = ring(y, -step)
        arrived(("z", step, "far"))
        to_core(step, z_place(ring(z, 2), q))

    def core_wait(step):
        arrived(("core", step))

    z2 = z_start(2)
    gather_relay("tok", tok_first, tok_g, x, FEATS, at_x)

    arrived(("ad",))
    holders = []
    for j in range(USED):
        holder = store_row[expert[j, seq]] // STORED
        rank = jnp.int32(0)
        for earlier in holders:
            rank = rank + (earlier == holder).astype(jnp.int32)
        holders.append(holder)
        rows = ad_recv[holder * CAP + rank]
        dd[pl.ds(j * RANK, RANK), cols_x] = rows[:, :FEATS]
        uu[pl.ds(j * RANK, RANK), cols_y] = rows[:, FEATS:]
    low_rows = pl.ds(0, LOW)
    low_half = (pl.ds(0, LOW // 2), pl.ds(LOW // 2, LOW // 2))
    up_first = []
    for way in (0, 1):
        here = uu.at[low_half[way], cols_y]
        up_first.append(remote(("up", way), here, here, at_y(1 - 2 * way)))
    for way in (0, 1):
        here = uu.at[low_half[1 - way], cols_y]
        remote(("up", "rest"), here, here, at_y(1 - 2 * way))
    cot_first = gather_first("cot", cot, cot_g, cols_y, at_y)
    for step in (2, 1, 3):
        here = dd.at[low_rows, cols_x]
        remote(("down",), here, here, at_x(step))

    z_relay(2, z2)
    z3 = z_start(3)
    z1 = z_start(1)
    for way in (0, 1):
        up_first[way].wait_recv()
        here = uu.at[low_half[way], ds(ring(y, 2 * way - 1) * COLS, COLS, 128)]
        remote(("up", "rest"), here, here, at_y(1 - 2 * way))
    gather_second("cot", cot, cot_g, cols_y, at_y)
    z_near(2)
    z_far(2)

    loads[2].wait()
    for j in range(USED):
        row = jnp.broadcast_to(gate_v[pl.ds(j, 1), :], (RANK, GROUP))
        gate_t[pl.ds(j * RANK, RANK), :] = row
        gate_t[pl.ds(LOW + j * RANK, RANK), :] = row
    gate[...] = gate_t[...].T
    first_half = lax.broadcasted_iota(jnp.int32, (GROUP, 2 * LOW), 1) < LOW

    def split_gated(value, out):
        gated = value * gate[...]
        high = gated.astype(BF16).astype(F32)
        out[...] = jnp.where(first_half, high, gated - high).astype(BF16)

    arrived(("tok", "second"))
    arrived(("tok", "relay"))
    loads[3].wait()
    gather_relay("cot", cot_first, cot_g, y, COLS, at_y)
    arrived(("down",))
    arrived(("up", "rest"))
    dd[LOW:, :] = dd[:LOW, :]
    uu[LOW:, :] = uu[:LOW, :]
    split_gated(
        lax.dot_general(tok_g[...], dd[...], TRANSPOSED, preferred_element_type=F32), low_hl
    )

    def project(q):
        cols = ds(q * COLS, COLS, 128)
        return jnp.dot(tok_g[...], wg[:, cols], preferred_element_type=F32) + jnp.dot(
            low_hl[...], uu[:, cols], preferred_element_type=F32
        )

    def input_grad(q):
        feats = ds(q * FEATS, FEATS, FEATS)
        return lax.dot_general(
            cot_g[...], wg[feats, :], TRANSPOSED, preferred_element_type=F32
        ) + jnp.dot(
            back_hl[...], dd[:, ds(q * FEATS, FEATS, 128)], preferred_element_type=F32
        )

    def far_send(name, value, far, relay, at):
        far[...] = value.astype(BF16)
        return [
            [
                remote((name, "f", way, k), far.at[chunk(way, k), :], relay.at[way, pl.ds(k * CHUNK, CHUNK), :], at(1 if way == 0 else -1))
                for k in range(CHUNKS)
            ]
            for way in (0, 1)
        ]

    def near_compute(value, way, out, keep):
        direct = 1 - way
        out[pl.ds(direct * HALF, HALF), :] = value[direct * HALF : (direct + 1) * HALF].astype(BF16)
        keep[way] = value[way * HALF : (way + 1) * HALF]

    def near_send(name, way, out, arrive, at):
        rows = [chunk(1 - way, k) for k in range(CHUNKS)]
        for row in rows:
            remote((name, "n", way), out.at[row, :], arrive.at[way, row, :], at(1 if way == 0 else -1))

    def relay_send(name, far_in, way, k, out, keep, relay, arrive, at):
        first, size = SUMS[k]
        if first % CHUNK == 0:
            far_in[way][first // CHUNK].wait_recv()
        inner = pl.ds(first, size)
        outer = pl.ds(way * HALF + first, size)
        out[outer, :] = (keep[way, inner, :] + relay[way, inner, :].astype(F32)).astype(BF16)
        return remote((name, "s", way, k), out.at[outer, :], arrive.at[way, outer, :], at(1 if way == 0 else -1))

    def finish(sums, way, k, own, arrive, out, result, sem):
        sums[way][k].wait_recv()
        first, size = SUMS[k]
        rows = pl.ds(way * HALF + first, size)
        out[rows, :] = (
            own[rows, :] + arrive[0, rows, :].astype(F32) + arrive[1, rows, :].astype(F32)
        ).astype(BF16)
        copy = pltpu.make_async_copy(out.at[rows, :], result.at[rows, :], local_sem.at[sem])
        copy.start()
        return copy

    x2_feats = ds(ring(x, 2) * FEATS, FEATS, FEATS)

    def back_of(q):
        cols = ds(q * COLS, COLS, 128)
        return lax.dot_general(cot_g[:, cols], uu[:, cols], TRANSPOSED, preferred_element_type=F32)

    def x2_of(q):
        cols = ds(q * COLS, COLS, 128)
        return lax.dot_general(cot_g[:, cols], wg[x2_feats, cols], TRANSPOSED, preferred_element_type=F32)

    core_wait(2)
    loads[5].wait()
    y_far_in = far_send("y", project(ring(y, 2)), y_far, y_relay, at_y)
    z_relay(3, z3)
    y_own[...] = project(y)
    z_near(3)
    z_relay(1, z1)
    loads[4].wait()
    x2_part[...] = x2_of(y)
    z_far(3)
    z_near(1)
    z_far(1)
    core_wait(3)
    arrived(("cot", "second"))
    back_part[...] = back_of(y) + back_of(ring(y, 1)) + back_of(ring(y, -1))
    x2_part[...] += x2_of(ring(y, 1))
    core_wait(1)
    x2_part[...] += x2_of(ring(y, -1))
    near_compute(project(ring(y, 1)), 0, y_plus, y_keep)

    arrived(("cot", "relay"))
    split_gated(back_part[...] + back_of(ring(y, 2)), back_hl)
    x2_value = x2_part[...] + x2_of(ring(y, 2)) + jnp.dot(
        back_hl[...], dd[:, ds(ring(x, 2) * FEATS, FEATS, 128)], preferred_element_type=F32
    )
    x_far_in = far_send("x", x2_value, x_far, x_relay, at_x)
    near_send("y", 0, y_plus, y_in, at_y)
    near_compute(project(ring(y, -1)), 1, y_minus, y_keep)
    near_send("y", 1, y_minus, y_in, at_y)
    near_compute(input_grad(ring(x, 1)), 0, x_plus, x_keep)
    near_send("x", 0, x_plus, x_in, at_x)
    near_compute(input_grad(ring(x, -1)), 1, x_minus, x_keep)
    near_send("x", 1, x_minus, x_in, at_x)
    x_own[...] = input_grad(x)
    y_sums, x_sums = ([], []), ([], [])
    for k in range(len(SUMS)):
        y_sums[0].append(relay_send("y", y_far_in, 0, k, y_plus, y_keep, y_relay, y_in, at_y))
        y_sums[1].append(relay_send("y", y_far_in, 1, k, y_minus, y_keep, y_relay, y_in, at_y))
        x_sums[0].append(relay_send("x", x_far_in, 0, k, x_plus, x_keep, x_relay, x_in, at_x))
        x_sums[1].append(relay_send("x", x_far_in, 1, k, x_minus, x_keep, x_relay, x_in, at_x))
    for name in ("x", "y"):
        for way in (0, 1):
            arrived((name, "n", way))
    last = []
    for k in range(len(SUMS)):
        for way in (0, 1):
            last.append(finish(x_sums, way, k, x_own, x_in, x_out, grad_tokens, len(loads) + len(last)))
        for way in (0, 1):
            last.append(finish(y_sums, way, k, y_own, y_in, y_out, projected, len(loads) + len(last)))
    for copy in last:
        copy.wait()
    for kind, size in sent.items():
        wait_for(kind, size, send_sem.at[send_index[kind]])
    assert len(send_index) == N_SEND and len(recv_index) == N_RECV


def copy_kernel(a, b, a_out, b_out, a_v, b_v, in_sems, out_sems):
    pairs = []
    for i, (src, held, dst) in enumerate(((a, a_v, a_out), (b, b_v, b_out))):
        for k in range(COPIES):
            rows = pl.ds(k * (GROUP // COPIES), GROUP // COPIES)
            pairs.append((
                pltpu.make_async_copy(src.at[rows, :], held.at[rows, :], in_sems.at[i, k]),
                pltpu.make_async_copy(held.at[rows, :], dst.at[rows, :], out_sems.at[i, k]),
            ))
    for fetch, _ in pairs:
        fetch.start()
    for fetch, store in pairs:
        fetch.wait()
        store.start()
    for _, store in pairs:
        store.wait()


def per_device(tokens, cotangent, gates, weight, down, up, expert, store_row):
    any_space = pl.BlockSpec(memory_space=pl.ANY)

    def ring_scratch(width):
        return [
            pltpu.VMEM((GROUP, width), BF16),
            pltpu.VMEM((GROUP, width), BF16),
            pltpu.VMEM((GROUP, width), BF16),
            pltpu.VMEM((2, HALF, width), F32),
            pltpu.VMEM((GROUP, width), F32),
            pltpu.VMEM((2, HALF, width), BF16),
            pltpu.VMEM((2, GROUP, width), BF16),
            pltpu.VMEM((GROUP, width), BF16),
        ]

    flops = 2 * 2 * GROUP * ROW_FEATS * ROW_COLS
    outs = (
        jax.ShapeDtypeStruct((GROUP, COLS), BF16),
        jax.ShapeDtypeStruct((GROUP, FEATS), BF16),
    )
    result = pl.pallas_call(
        kernel,
        out_shape=outs,
        in_specs=[any_space] * 8,
        out_specs=(any_space, any_space),
        scratch_shapes=[
            pltpu.VMEM((ROW_FEATS, ROW_COLS), BF16),
            pltpu.VMEM((GROUP, ROW_FEATS), BF16),
            pltpu.VMEM((GROUP, ROW_COLS), BF16),
            pltpu.VMEM((USED, GROUP), F32),
            pltpu.VMEM((2 * LOW, GROUP), F32),
            pltpu.VMEM((GROUP, 2 * LOW), F32),
            pltpu.VMEM((STORED, RANK, FEATS), BF16),
            pltpu.VMEM((STORED, RANK, COLS), BF16),
            pltpu.VMEM((SEQ * CAP, RANK, FEATS + COLS), BF16),
            pltpu.VMEM((SEQ * CAP, RANK, FEATS + COLS), BF16),
            pltpu.VMEM((2 * LOW, ROW_FEATS), BF16),
            pltpu.VMEM((2 * LOW, ROW_COLS), BF16),
            pltpu.VMEM((GROUP, 2 * LOW), BF16),
            pltpu.VMEM((GROUP, 2 * LOW), BF16),
            pltpu.VMEM((GROUP, 2 * LOW), F32),
            pltpu.VMEM((GROUP, FEATS), F32),
        ]
        + ring_scratch(COLS)
        + ring_scratch(FEATS)
        + [
            pltpu.SMEM((USED, SEQ), jnp.int32),
            pltpu.SMEM((SEQ * STORED,), jnp.int32),
            pltpu.SemaphoreType.DMA((8 + 4 * len(SUMS),)),
            pltpu.SemaphoreType.DMA((N_SEND,)),
            pltpu.SemaphoreType.DMA((N_RECV,)),
        ],
        compiler_params=pltpu.CompilerParams(
            collective_id=0, has_side_effects=True, vmem_limit_bytes=60 * 2**20
        ),
        cost_estimate=pl.CostEstimate(flops=flops, bytes_accessed=20 * 2**20, transcendentals=0),
        name="mixture",
    )(tokens, cotangent, gates.T, weight, down, up, expert.T, store_row)
    return pl.pallas_call(
        copy_kernel,
        out_shape=outs,
        in_specs=[any_space] * 2,
        out_specs=(any_space, any_space),
        scratch_shapes=[
            pltpu.VMEM((GROUP, COLS), BF16),
            pltpu.VMEM((GROUP, FEATS), BF16),
            pltpu.SemaphoreType.DMA((2, COPIES)),
            pltpu.SemaphoreType.DMA((2, COPIES)),
        ],
        compiler_params=pltpu.CompilerParams(vmem_limit_bytes=60 * 2**20),
        name="results",
    )(*result)


def solution(mesh):
    return jax.shard_map(
        per_device,
        mesh=mesh,
        in_specs=(
            P("seq", "tensor"),
            P("seq", "tensor"),
            P("seq", None),
            P(None, "tensor"),
            P("seq", None, "tensor"),
            P("seq", None, "tensor"),
            P(),
            P(),
        ),
        out_specs=(P("seq", "tensor"), P("seq", "tensor")),
        check_vma=False,
    )
```
